32 devices in a mesh: blk: 8 (over z, y), inner: 4 (over x, core).
Axes of the slice: x: 2, y: 2, z: 4, core: 2. Of those that a mesh axis runs over, the one named last changes fastest.
Arguments:
- density: float32 [64, 9, 128, 128], P(('blk', 'inner')), may hold values from -0.5 to 0.5
- block_cols: int32 [64, 9], P(('blk', 'inner')), may hold values from 0 to 63, as said below
- targets: int32 [64, 9, 9], P(('blk', 'inner')), may hold values from 0 to 9, as said below
Outputs:
- purified: float32 [64, 9, 128, 128], P(('blk', 'inner'))
The draws below stay inside these ranges and needn't reach their ends.
Inputs may be any that keep to these rules, and one draw needn't show every extreme that they name: `block_cols`: strips are runs of 8 block rows. Slots 0 .. 2, 3 .. 5 and 6 .. 8 of row k hold 3 distinct columns each, ascending, from the strip before k's own (cyclically), k's own strip, and the strip after it (cyclically); the own group always contains column k. targets[k, s, t] is the slot u with block_cols[block_cols[k, s], u] == block_cols[k, t], or 9 where row block_cols[k, s] does not store that column.
All inputs are finite; a program needn't handle non-finite values.
Results may differ from the reference program's by a relative error of at most 0.0001.
Values sent between devices are 32-bit elements; how exact they have to be, the bound alone decides.
No kernel may reach another device: no remote copies, remote signals or barrier semaphores. Data moves between devices by JAX's collectives and lax.ppermute only.
A program may use at most 128 MiB of HBM per device.

```python
import jax
import jax.numpy as jnp
from jax import lax

B = 128
STRIP = 8
PER = 3
NZ = 9
NB = 64


def pattern(key):
    base_key = jax.random.fold_in(key, 7)
    strips = NB // STRIP
    row_ids = jnp.arange(NB, dtype=jnp.int32)
    home_strip = row_ids // STRIP
    own_slot = row_ids % STRIP
    scores = jax.random.randint(base_key, (NB, 3, STRIP), 0, 1 << 20)
    unique_entries = scores * STRIP + jnp.arange(STRIP, dtype=jnp.int32)[None, None, :]
    forced = (jnp.arange(3)[None, :, None] == 1) & (jnp.arange(STRIP)[None, None, :] == own_slot[:, None, None])
    unique_entries = jnp.where(forced, -1, unique_entries)
    ranked = jnp.argsort(unique_entries, axis=-1)[:, :, :PER]
    chosen = jnp.sort(ranked, axis=-1).astype(jnp.int32)
    strip_of = (home_strip[:, None] + jnp.arange(-1, 2, dtype=jnp.int32)[None, :]) % strips
    block_cols = (strip_of[:, :, None] * STRIP + chosen).reshape(NB, NZ).astype(jnp.int32)
    neighbour_cols = block_cols[block_cols]
    matches = neighbour_cols[:, :, None, :] == block_cols[:, None, :, None]
    present = jnp.any(matches, axis=-1)
    slot_index = jnp.sum(jnp.where(matches, jnp.arange(NZ, dtype=jnp.int32), 0), axis=-1)
    targets = jnp.where(present, slot_index, NZ).astype(jnp.int32)
    return (block_cols, targets)


def draw_block_cols(key, part):
    return pattern(key)[0]


def draw_targets(key, part):
    return pattern(key)[1]


def block_levels(own_key, dims, cuts, smallest, largest):
    level, own = 1.0, jax.random.fold_in(own_key, 6)
    for position, blocks in cuts:
        heights = jnp.exp(jax.random.uniform(jax.random.fold_in(own, position), (blocks,), jnp.float32, smallest / len(cuts), largest / len(cuts)))
        level = level * jnp.repeat(heights, dims[position] // blocks).reshape([-1 if axis == position else 1 for axis in range(len(dims))])
    return level


def bell_draw(stream_key, shape, deviation, most, shards=(), held_as=jnp.bfloat16):
    entries = deviation * jax.random.normal(stream_key, shape, jnp.float32)
    if shards:
        entries = entries * block_levels(stream_key, shape, shards, -0.22, 0.18)
    return jnp.clip(entries, -most, most).astype(held_as)


def setup_inputs(seed: int = 0) -> dict:
    keys = jax.random.split(jax.random.key(seed), 4)
    return {
        "density": bell_draw(keys[0], (NB, NZ, B, B), 0.08, 0.5, ((0, 32),), jnp.float32),
        "block_cols": draw_block_cols(jax.random.fold_in(keys[3], 71), 0),
        "targets": draw_targets(jax.random.fold_in(keys[3], 71), 0),
    }


def reference(density, block_cols, targets):
    row_total, slot_total, block_side, _ = density.shape

    def accumulate_row(row_position_index, square):
        matrix_blocks = density[row_position_index]
        block_products = jnp.einsum("rzd,wzg->rwdg", matrix_blocks, matrix_blocks, precision=lax.Precision.HIGHEST)
        destination_rows = jnp.broadcast_to(block_cols[row_position_index][:, None], (slot_total, slot_total))
        dest_slots = targets[row_position_index]
        return square.at[destination_rows, dest_slots].add(block_products, mode="drop")

    square = lax.fori_loop(0, row_total, accumulate_row, jnp.zeros_like(density))
    return 2.0 * density - square
```

```python
import jax
import jax.numpy as jnp
from jax import lax
from jax.experimental import pallas as pl
from jax.experimental.pallas import tpu as pltpu
from jax.sharding import PartitionSpec as P

TN = (((0,), (0,)), ((), ()))


def shifted(value, steps):
    count = lax.axis_size("blk")
    pairs = [(source, (source + steps) % count) for source in range(count)]
    return lax.ppermute(value, "blk", pairs)


def swapped(value, distance):
    count = lax.axis_size("inner")
    return lax.ppermute(value, "inner", [(i, i ^ distance) for i in range(count)])


def gathered(value):
    count = lax.axis_size("inner")
    held = {0: value}
    bit = count // 2
    while bit:
        for distance in list(held):
            held[distance ^ bit] = swapped(held[distance], bit)
        bit //= 2
    return [held[distance] for distance in range(count)]


def products_kernel(dims, *refs):
    parts, local_rows, slots, side = dims
    per = slots // 3
    data = local_rows * slots * side
    payloads = refs[:parts]
    up_out, own_out, down_out = refs[parts : parts + 3]
    split, codes_v, codes, listed, up, own, down, meta_sem, out_sems = refs[parts + 3 :]

    for part in range(parts):
        codes_v[part] = payloads[part][data:, :].astype(jnp.int32)
    fetch = pltpu.make_async_copy(codes_v, codes, meta_sem)
    fetch.start()
    for acc in (up, own, down):
        acc[...] = jnp.zeros_like(acc)
    for part in range(parts):

        def cut(row, _, part=part):
            for slot in range(slots):
                start = pl.multiple_of((row * slots + slot) * side, side)
                block = payloads[part][pl.ds(start, side), :]
                high = block.astype(jnp.bfloat16)
                low = (block - high.astype(jnp.float32)).astype(jnp.bfloat16)
                lanes = slice(slot * side, (slot + 1) * side)
                split[part * local_rows + row, :side, lanes] = high
                split[part * local_rows + row, side:, lanes] = low
            return 0

        lax.fori_loop(0, local_rows, cut, 0)
    fetch.wait()

    plans = (
        (2, up, 0, 2 * per, per, slots),
        (1, own, 0, slots, 0, slots),
        (0, down, per, 2 * per, 0, 2 * per),
    )
    for index, (group, acc, first, width, low_t, high_t) in enumerate(plans):

        def collect(row, count, group=group):
            part, line = row // local_rows, lax.rem(row, local_rows)
            for slot in range(group * per, (group + 1) * per):
                dest = codes[part, line, slot] - part * local_rows
                mine = (dest >= 0) & (dest < local_rows)

                @pl.when(mine)
                def _():
                    listed[0, count] = row
                    listed[1, count] = slot
                    listed[2, count] = dest

                count = count + mine.astype(jnp.int32)
            return count

        total = lax.fori_loop(0, parts * local_rows, collect, 0)

        def multiply(item, _, acc=acc, first=first, width=width, low_t=low_t, high_t=high_t):
            row, slot, dest = listed[0, item], listed[1, item], listed[2, item]
            part, line = row // local_rows, lax.rem(row, local_rows)
            lanes = pl.ds(pl.multiple_of(slot * side, side), side)
            a_high = split[row, :side, lanes]
            a_low = split[row, side:, lanes]
            span = slice(low_t * side, high_t * side)
            b_high = split[row, :side, span]
            b_low = split[row, side:, span]
            dot = lambda x, y: lax.dot_general(x, y, TN, preferred_element_type=jnp.float32)
            result = dot(a_high, b_high) + (dot(a_high, b_low) + dot(a_low, b_high))
            for t in range(low_t, high_t):
                target = codes[part, line, slots + slot * slots + t]
                place = jnp.minimum(target - first, width)
                at = (t - low_t) * side
                acc[dest, place] += result[:, at : at + side]
            return 0

        lax.fori_loop(0, total, multiply, 0)
        out = (up_out, own_out, down_out)[index]
        pltpu.make_async_copy(acc.at[:, :width], out, out_sems.at[index]).start()
    for index, (group, acc, first, width, low_t, high_t) in enumerate(plans):
        out = (up_out, own_out, down_out)[index]
        pltpu.make_async_copy(acc.at[:, :width], out, out_sems.at[index]).wait()


def shards(density, block_cols, targets):
    local_rows, slots, side, _ = density.shape
    per = slots // 3
    parts = lax.axis_size("inner")
    strip_rows = local_rows * parts
    inner = lax.axis_index("inner")

    in_strip = block_cols % strip_rows
    codes = ((in_strip // local_rows) ^ inner) * local_rows + in_strip % local_rows
    codes = jnp.concatenate([codes, targets.reshape(local_rows, slots * slots)], axis=1)
    codes = jnp.pad(codes.astype(jnp.float32), ((0, -local_rows % 8), (0, side - codes.shape[1])))
    meta_rows = codes.shape[0]
    payload = jnp.concatenate([density.reshape(-1, side), codes], axis=0)
    payloads = gathered(payload)

    half = jax.ShapeDtypeStruct((local_rows, 2 * per, side, side), jnp.float32)
    full = jax.ShapeDtypeStruct(density.shape, jnp.float32)
    up, own, down = pl.pallas_call(
        lambda *refs: products_kernel((parts, local_rows, slots, side), *refs),
        out_shape=(half, full, half),
        in_specs=[pl.BlockSpec(memory_space=pltpu.VMEM)] * parts,
        out_specs=[pl.BlockSpec(memory_space=pl.ANY)] * 3,
        scratch_shapes=[
            pltpu.VMEM((strip_rows, 2 * side, slots * side), jnp.bfloat16),
            pltpu.VMEM((parts, meta_rows, side), jnp.int32),
            pltpu.SMEM((parts, meta_rows, side), jnp.int32),
            pltpu.SMEM((3, strip_rows * per), jnp.int32),
            pltpu.VMEM((local_rows, 2 * per + 1, side, side), jnp.float32),
            pltpu.VMEM((local_rows, slots + 1, side, side), jnp.float32),
            pltpu.VMEM((local_rows, 2 * per + 1, side, side), jnp.float32),
            pltpu.SemaphoreType.DMA,
            pltpu.SemaphoreType.DMA((3,)),
        ],
        compiler_params=pltpu.CompilerParams(vmem_limit_bytes=48 << 20),
        cost_estimate=pl.CostEstimate(flops=10**9, bytes_accessed=8 << 20, transcendentals=0),
        name="strip_products",
    )(*payloads)
    from_below = shifted(up, 1)
    from_above = shifted(down, -1)
    square = own.at[:, : 2 * per].add(from_below)
    square = square.at[:, per:].add(from_above)
    return 2.0 * density - square


def solution(mesh):
    return jax.shard_map(
        shards,
        mesh=mesh,
        in_specs=(
            P(("blk", "inner"), None, None, None),
            P(("blk", "inner"), None),
            P(("blk", "inner"), None, None),
        ),
        out_specs=P(("blk", "inner"), None, None, None),
        check_vma=False,
    )
```

```python
import functools

import jax
import jax.numpy as jnp
from jax import lax
from jax.experimental import pallas as pl
from jax.experimental.pallas import tpu as pltpu
from jax.sharding import PartitionSpec as P

TN = (((0,), (0,)), ((), ()))


def shifted(value, steps):
    count = lax.axis_size("blk")
    pairs = [(source, (source + steps) % count) for source in range(count)]
    return lax.ppermute(value, "blk", pairs)


def swapped(value, distance):
    count = lax.axis_size("inner")
    return lax.ppermute(value, "inner", [(i, i ^ distance) for i in range(count)])


def gathered(value, after=None):
    count = lax.axis_size("inner")
    held = {0: value}
    bit = count // 2
    farthest = None
    while bit:
        for distance in list(held):
            operand = held[distance]
            if farthest is None and after is not None:
                operand, _ = lax.optimization_barrier((operand, after))
            held[distance ^ bit] = swapped(operand, bit)
            if farthest is None:
                farthest = held[distance ^ bit]
        bit //= 2
    return [held[distance] for distance in range(count)], farthest


def pack_kernel(dims, density, targets, cols, inner, *refs):
    local_rows, slots, side, strip_rows, meta_rows = dims
    per = slots // 3
    data = local_rows * per * side
    outs, (meta, sems) = refs[:3], refs[3:]
    copies = []
    for group in (0, 2, 1):
        for row in range(local_rows):
            source = density.at[pl.ds((row * slots + group * per) * side, per * side)]
            dest = outs[group].at[pl.ds(row * per * side, per * side)]
            copies.append(pltpu.make_async_copy(source, dest, sems.at[group, row]))
            copies[-1].start()
    meta[...] = jnp.zeros_like(meta)
    lines = lax.broadcasted_iota(jnp.int32, (per, 1), 0)
    for group in (0, 2, 1):
        for row in range(local_rows):
            column = jnp.zeros((per, 1), jnp.int32)
            for slot in range(per):
                in_strip = lax.rem(cols[row, group * per + slot], strip_rows)
                owner = lax.div(in_strip, local_rows) ^ inner[0]
                code = owner * local_rows + lax.rem(in_strip, local_rows)
                column = jnp.where(lines == slot, code, column)
            span = slice(row * per, (row + 1) * per)
            chosen = targets[row, group * per : (group + 1) * per, :]
            meta[group, span, :slots] = chosen.astype(jnp.float32)
            meta[group, span, slots : slots + 1] = column.astype(jnp.float32)
        dest = outs[group].at[pl.ds(data, meta_rows)]
        copies.append(pltpu.make_async_copy(meta.at[group], dest, sems.at[group, local_rows]))
        copies[-1].start()
    for copy in copies:
        copy.wait()


def sums_kernel(dims, plan, *refs):
    parts, local_rows, slots, side, meta_rows, a_at, group_total, first, width, final = dims
    per = slots // 3
    data = local_rows * per * side
    payloads = [refs[g * parts : (g + 1) * parts] for g in range(group_total)]
    out, raw, meta, listed, acc, sems, meta_sems, out_sem = refs[group_total * parts :]

    fetches = []
    for part in range(parts):
        source = payloads[a_at][part].at[pl.ds(data, meta_rows)]
        fetches.append(pltpu.make_async_copy(source, meta.at[part], meta_sems.at[part]))
        fetches[-1].start()
    loads = []
    for group in range(group_total):
        for part in range(parts):
            source = payloads[group][part].at[pl.ds(0, data)]
            loads.append(pltpu.make_async_copy(source, raw.at[group, part], sems.at[group, part]))
            loads[-1].start()
    acc[...] = jnp.zeros_like(acc)
    for fetch in fetches:
        fetch.wait()

    count = jnp.int32(0)
    for part in range(parts):
        for line in range(local_rows * per):
            dest = meta[part, line, slots].astype(jnp.int32) - part * local_rows
            listed[0, count] = part
            listed[1, count] = line
            listed[2, count] = dest
            mine = (dest >= 0) & (dest < local_rows)
            count = count + mine.astype(jnp.int32)
    for load in loads:
        load.wait()

    def cut(block):
        high = block.astype(jnp.bfloat16)
        return high, (block - high.astype(jnp.float32)).astype(jnp.bfloat16)

    def multiply(item, _):
        part, line, dest = listed[0, item], listed[1, item], listed[2, item]
        row = lax.div(line, per)
        start = pl.multiple_of(line * side, side)
        a_high, a_low = cut(raw[a_at, part, pl.ds(start, side), :])
        a = jnp.concatenate([a_high, a_high, a_low], axis=0)
        for group, lane in plan:
            blocks = []
            for t in range(per):
                start = pl.multiple_of((row * per + t) * side, side)
                blocks.append(raw[group, part, pl.ds(start, side), :])
            b_high, b_low = cut(jnp.concatenate(blocks, axis=1))
            b = jnp.concatenate([b_high, b_low, b_high], axis=0)
            result = lax.dot_general(a, b, TN, preferred_element_type=jnp.float32)
            for t in range(per):
                target = meta[part, line, lane + t].astype(jnp.int32)
                place = jnp.minimum(target - first, width)
                acc[dest, place] += result[:, t * side : (t + 1) * side]
        return 0

    lax.fori_loop(0, count, multiply, 0)
    if final:
        for row in range(local_rows):
            for t in range(slots):
                start = (row * per + t % per) * side
                mine = raw[t // per, 0, start : start + side, :]
                acc[row, t] = 2.0 * mine - acc[row, t]
    copy = pltpu.make_async_copy(acc.at[:, :width], out, out_sem)
    copy.start()
    copy.wait()


def shards(density, block_cols, targets):
    local_rows, slots, side, _ = density.shape
    per = slots // 3
    parts = lax.axis_size("inner")
    strip_rows = local_rows * parts
    meta_rows = local_rows * per + -(local_rows * per) % 8
    payload_rows = local_rows * per * side + meta_rows
    anywhere = pl.BlockSpec(memory_space=pl.ANY)
    scalars = pl.BlockSpec(memory_space=pltpu.SMEM)

    packed = pl.pallas_call(
        functools.partial(pack_kernel, (local_rows, slots, side, strip_rows, meta_rows)),
        out_shape=[jax.ShapeDtypeStruct((payload_rows, side), jnp.float32)] * 3,
        in_specs=[anywhere, pl.BlockSpec(memory_space=pltpu.VMEM), scalars, scalars],
        out_specs=[anywhere] * 3,
        scratch_shapes=[
            pltpu.VMEM((3, meta_rows, side), jnp.float32),
            pltpu.SemaphoreType.DMA((3, local_rows + 1)),
        ],
        name="pack",
    )(density.reshape(-1, side), targets, block_cols, lax.axis_index("inner").reshape(1))

    def sums(groups, a_at, plan, first, width, final=False):
        dims = (parts, local_rows, slots, side, meta_rows, a_at, len(groups), first, width, final)
        work = 3 * 2 * side**3 * strip_rows * per * per * len(plan)
        return pl.pallas_call(
            functools.partial(sums_kernel, dims, plan),
            out_shape=jax.ShapeDtypeStruct((local_rows, width, side, side), jnp.float32),
            in_specs=[anywhere] * (parts * len(groups)),
            out_specs=anywhere,
            scratch_shapes=[
                pltpu.VMEM((len(groups), parts, local_rows * per * side, side), jnp.float32),
                pltpu.SMEM((parts, meta_rows, side), jnp.float32),
                pltpu.SMEM((3, strip_rows * per + 1), jnp.int32),
                pltpu.VMEM((local_rows, width + 1, side, side), jnp.float32),
                pltpu.SemaphoreType.DMA((len(groups), parts)),
                pltpu.SemaphoreType.DMA((parts,)),
                pltpu.SemaphoreType.DMA,
            ],
            compiler_params=pltpu.CompilerParams(vmem_limit_bytes=32 << 20),
            cost_estimate=pl.CostEstimate(
                flops=work, bytes_accessed=len(groups) * density.size * 4, transcendentals=0
            ),
            name="sums",
        )(*[payload for group in groups for payload in group])

    lower, middle, upper = packed
    below = shifted(upper, 1)
    lower, last = gathered(lower)
    to_above_own = shifted(sums([lower], 0, ((0, 0),), per, per), -1)
    middle, last = gathered(middle, last)
    to_above_next = shifted(sums([lower, middle], 0, ((1, per),), 2 * per, per), -1)
    upper, last = gathered(upper, last)
    to_below = shifted(sums([upper, middle], 0, ((1, per),), 0, per), 1)
    below, last = gathered(below, last)
    own_plan = ((0, 0), (1, per), (2, 2 * per))
    base = sums([lower, middle, upper], 1, own_plan, 0, slots, True)
    from_below = sums([below], 0, ((0, 2 * per),), per, per)
    received = [to_below, to_above_own + from_below, to_above_next]
    return base - jnp.concatenate(received, axis=1)


def solution(mesh):
    return jax.shard_map(
        shards,
        mesh=mesh,
        in_specs=(
            P(("blk", "inner"), None, None, None),
            P(("blk", "inner"), None),
            P(("blk", "inner"), None, None),
        ),
        out_specs=P(("blk", "inner"), None, None, None),
        check_vma=False,
    )
```

```python
import functools

import jax
import jax.numpy as jnp
from jax import lax
from jax.experimental import pallas as pl
from jax.experimental.pallas import tpu as pltpu
from jax.sharding import PartitionSpec as P

TN = (((0,), (0,)), ((), ()))


def shifted(value, steps):
    count = lax.axis_size("blk")
    pairs = [(source, (source + steps) % count) for source in range(count)]
    return lax.ppermute(value, "blk", pairs)


def swapped(value, distance):
    count = lax.axis_size("inner")
    return lax.ppermute(value, "inner", [(i, i ^ distance) for i in range(count)])


def halves(value):
    held = [value]
    for bit in [1 << i for i in range(20) if (1 << i) < lax.axis_size("inner") // 2]:
        held = held + [swapped(one, bit) for one in held]
    return held


def across(value, after=()):
    count = lax.axis_size("inner")
    value = lax.optimization_barrier((value, *after))[0] if after else value
    return [swapped(value, count // 2)] if count > 1 else []


def parted(value, size):
    if size & (size - 1) == 0:
        return value >> (size.bit_length() - 1), value & (size - 1)
    return lax.div(value, size), lax.rem(value, size)


def pack_kernel(dims, density, targets, cols, inner, *refs):
    local_rows, slots, side, strip_rows, meta_rows = dims
    per = slots // 3
    data = local_rows * per * side
    outs, sems = refs[:3], refs[3]
    copies = []
    for group in (0, 2, 1):
        for row in range(local_rows):
            source = density.at[pl.ds((row * slots + group * per) * side, per * side)]
            dest = outs[group].at[pl.ds(row * per * side, per * side)]
            copies.append(pltpu.make_async_copy(source, dest, sems.at[group, row]))
            copies[-1].start()
    for group in (0, 2, 1):
        outs[group][data:, :] = jnp.zeros((meta_rows, side), jnp.float32)
        for row in range(local_rows):
            for slot in range(per):
                in_strip = parted(cols[row, group * per + slot], strip_rows)[1]
                owner, line = parted(in_strip, local_rows)
                code = (owner ^ inner[0]) * local_rows + line
                at = data + row * per + slot
                chosen = targets[group * per + slot, row : row + 1, :]
                outs[group][at : at + 1, :slots] = chosen.astype(jnp.float32)
                code = jnp.full((1, 1), code, jnp.int32).astype(jnp.float32)
                outs[group][at : at + 1, slots : slots + 1] = code
    for copy in copies:
        copy.wait()


def sums_kernel(dims, plan, *refs):
    parts, local_rows, slots, side, meta_rows, a_at, group_total, first, width, final = dims
    per = slots // 3
    data = local_rows * per * side
    payloads = [refs[g * parts : (g + 1) * parts] for g in range(group_total)]
    out, meta, listed, acc, meta_sems = refs[group_total * parts :]

    fetches = []
    for part in range(parts):
        source = payloads[a_at][part].at[pl.ds(data, meta_rows)]
        fetches.append(pltpu.make_async_copy(source, meta.at[part], meta_sems.at[part]))
        fetches[-1].start()
    acc[...] = jnp.zeros_like(acc)

    def cut(block):
        high = block.astype(jnp.bfloat16)
        return high, (block - high.astype(jnp.float32)).astype(jnp.bfloat16)

    for part in range(parts):
        fetches[part].wait()
        count = jnp.int32(0)
        for line in range(local_rows * per):
            dest = meta[part, line, slots].astype(jnp.int32) - part * local_rows
            listed[0, count] = line
            listed[1, count] = line // per
            listed[2, count] = dest
            mine = (dest >= 0) & (dest < local_rows)
            count = count + mine.astype(jnp.int32)

        def multiply(item, _, part=part):
            line, row, dest = listed[0, item], listed[1, item], listed[2, item]
            start = pl.multiple_of(line * side, side)
            a_high, a_low = cut(payloads[a_at][part][pl.ds(start, side), :])
            a = jnp.concatenate([a_high, a_high, a_low], axis=0)
            for group, lane in plan:
                blocks = []
                for t in range(per):
                    start = pl.multiple_of((row * per + t) * side, side)
                    blocks.append(payloads[group][part][pl.ds(start, side), :])
                b_high, b_low = cut(jnp.concatenate(blocks, axis=1))
                b = jnp.concatenate([b_high, b_low, b_high], axis=0)
                result = lax.dot_general(a, b, TN, preferred_element_type=jnp.float32)
                for t in range(per):
                    target = meta[part, line, lane + t].astype(jnp.int32)
                    place = jnp.minimum(target - first, width)
                    acc[dest, place] += result[:, t * side : (t + 1) * side]
            return 0

        lax.fori_loop(0, count, multiply, 0)
    for row in range(local_rows):
        for t in range(width):
            if final:
                start = (row * per + t % per) * side
                mine = payloads[t // per][0][start : start + side, :]
                out[row, t] = 2.0 * mine - acc[row, t]
            else:
                out[row, t] = acc[row, t]


def shards(density, block_cols, targets):
    local_rows, slots, side, _ = density.shape
    per = slots // 3
    parts = lax.axis_size("inner")
    strip_rows = local_rows * parts
    meta_rows = local_rows * per + -(local_rows * per) % 8
    payload_rows = local_rows * per * side + meta_rows
    anywhere = pl.BlockSpec(memory_space=pl.ANY)
    scalars = pl.BlockSpec(memory_space=pltpu.SMEM)
    vectors = pl.BlockSpec(memory_space=pltpu.VMEM)

    lower, middle, upper = pl.pallas_call(
        functools.partial(pack_kernel, (local_rows, slots, side, strip_rows, meta_rows)),
        out_shape=[jax.ShapeDtypeStruct((payload_rows, side), jnp.float32)] * 3,
        in_specs=[anywhere, vectors, scalars, scalars],
        out_specs=[vectors] * 3,
        scratch_shapes=[pltpu.SemaphoreType.DMA((3, local_rows))],
        compiler_params=pltpu.CompilerParams(vmem_limit_bytes=8 << 20),
        name="pack",
    )(
        density.reshape(-1, side),
        jnp.transpose(targets, (1, 0, 2)),
        block_cols,
        lax.axis_index("inner").reshape(1),
    )

    def sums(groups, a_at, plan, first, width, final=False):
        dims = (parts, local_rows, slots, side, meta_rows, a_at, len(groups), first, width, final)
        work = 3 * 2 * side**3 * strip_rows * per * per * len(plan)
        return pl.pallas_call(
            functools.partial(sums_kernel, dims, plan),
            out_shape=jax.ShapeDtypeStruct((local_rows, width, side, side), jnp.float32),
            in_specs=[vectors] * (parts * len(groups)),
            out_specs=vectors,
            scratch_shapes=[
                pltpu.SMEM((parts, meta_rows, side), jnp.float32),
                pltpu.SMEM((3, local_rows * per + 1), jnp.int32),
                pltpu.VMEM((local_rows, width + 1, side, side), jnp.float32),
                pltpu.SemaphoreType.DMA((parts,)),
            ],
            compiler_params=pltpu.CompilerParams(vmem_limit_bytes=16 << 20),
            cost_estimate=pl.CostEstimate(
                flops=work, bytes_accessed=len(groups) * density.size * 4, transcendentals=0
            ),
            name="sums",
        )(*[payload for group in groups for payload in group])

    below = shifted(upper, 1)
    lowers, middles, uppers = halves(lower), halves(middle), halves(upper)
    far_lower = across(lower)
    far_middle = across(middle, [below, *far_lower, *lowers, *middles, *uppers])
    lowers += [one for value in far_lower for one in halves(value)]
    above_own = sums([lowers], 0, ((0, 0),), per, per)
    to_above_own = shifted(above_own, -1)

    far_upper = across(upper, [*far_middle, above_own])
    middles += [one for value in far_middle for one in halves(value)]
    above_next = sums([lowers, middles], 0, ((1, per),), 2 * per, per)
    to_above_next = shifted(above_next, -1)

    far_below = across(below, [*far_upper, above_next, to_above_own])
    belows = halves(below)
    uppers += [one for value in far_upper for one in halves(value)]
    to_next = sums([uppers, middles], 0, ((1, per),), 0, per)
    to_below = shifted(to_next, 1)
    own_plan = ((0, 0), (1, per), (2, 2 * per))
    base = sums([lowers, middles, uppers], 1, own_plan, 0, slots, True)

    if far_below:
        far_below = [lax.optimization_barrier((far_below[0], to_next, base, *belows))[0]]
    belows += [one for value in far_below for one in halves(value)]
    from_below = sums([belows], 0, ((0, 2 * per),), per, per)
    received = [to_below, to_above_own + from_below, to_above_next]
    return base - jnp.concatenate(received, axis=1)


def solution(mesh):
    return jax.shard_map(
        shards,
        mesh=mesh,
        in_specs=(
            P(("blk", "inner"), None, None, None),
            P(("blk", "inner"), None),
            P(("blk", "inner"), None, None),
        ),
        out_specs=P(("blk", "inner"), None, None, None),
        check_vma=False,
    )
```

```python
import functools

import jax
import jax.numpy as jnp
from jax import lax
from jax.experimental import pallas as pl
from jax.experimental.pallas import tpu as pltpu
from jax.sharding import PartitionSpec as P

TN = (((0,), (0,)), ((), ()))


def shifted(value, steps):
    count = lax.axis_size("blk")
    pairs = [(source, (source + steps) % count) for source in range(count)]
    return lax.ppermute(value, "blk", pairs)


def swapped(value, distance):
    count = lax.axis_size("inner")
    return lax.ppermute(value, "inner", [(i, i ^ distance) for i in range(count)])


def halves(value):
    held = [value]
    for bit in [1 << i for i in range(20) if (1 << i) < lax.axis_size("inner") // 2]:
        held = held + [swapped(one, bit) for one in held]
    return held


def across(value, after=()):
    count = lax.axis_size("inner")
    value = lax.optimization_barrier((value, *after))[0] if after else value
    return [swapped(value, count // 2)] if count > 1 else []


def parted(value, size):
    if size & (size - 1) == 0:
        return value >> (size.bit_length() - 1), value & (size - 1)
    return lax.div(value, size), lax.rem(value, size)


def pack_kernel(dims, density, targets, cols, inner, *refs):
    local_rows, slots, side, strip_rows, meta_rows = dims
    per = slots // 3
    data = local_rows * per * side
    outs, sems = refs[:3], refs[3]
    copies = []
    for group in (0, 2, 1):
        for row in range(local_rows):
            source = density.at[pl.ds((row * slots + group * per) * side, per * side)]
            dest = outs[group].at[pl.ds(row * per * side, per * side)]
            copies.append(pltpu.make_async_copy(source, dest, sems.at[group, row]))
            copies[-1].start()
    for group in (0, 2, 1):
        outs[group][data:, :] = jnp.zeros((meta_rows, side), jnp.float32)
        for row in range(local_rows):
            for slot in range(per):
                in_strip = parted(cols[row, group * per + slot], strip_rows)[1]
                owner, line = parted(in_strip, local_rows)
                code = (owner ^ inner[0]) * local_rows + line
                at = data + row * per + slot
                chosen = targets[group * per + slot, row : row + 1, :]
                outs[group][at : at + 1, :slots] = chosen.astype(jnp.float32)
                code = jnp.full((1, 1), code, jnp.int32).astype(jnp.float32)
                outs[group][at : at + 1, slots : slots + 1] = code
    for copy in copies:
        copy.wait()


def sums_kernel(dims, plan, *refs):
    offset, parts, local_rows, slots, side, meta_rows, a_at, group_total, first, width = dims
    per = slots // 3
    data = local_rows * per * side
    payloads = [refs[g * parts : (g + 1) * parts] for g in range(group_total)]
    *base, out, meta, listed, acc, meta_sems = refs[group_total * parts :]

    fetches = []
    for part in range(parts):
        source = payloads[a_at][part].at[pl.ds(data, meta_rows)]
        fetches.append(pltpu.make_async_copy(source, meta.at[part], meta_sems.at[part]))
        fetches[-1].start()
    acc[...] = jnp.zeros_like(acc)

    def cut(block):
        high = block.astype(jnp.bfloat16)
        return high, (block - high.astype(jnp.float32)).astype(jnp.bfloat16)

    for part in range(parts):
        fetches[part].wait()
        count = jnp.int32(0)
        for line in range(local_rows * per):
            dest = meta[part, line, slots].astype(jnp.int32) - (offset + part) * local_rows
            listed[0, count] = line
            listed[1, count] = line // per
            listed[2, count] = dest
            mine = (dest >= 0) & (dest < local_rows)
            count = count + mine.astype(jnp.int32)

        def multiply(item, _, part=part):
            line, row, dest = listed[0, item], listed[1, item], listed[2, item]
            start = pl.multiple_of(line * side, side)
            a_high, a_low = cut(payloads[a_at][part][pl.ds(start, side), :])
            a = jnp.concatenate([a_high, a_high, a_low], axis=0)
            for group, lane in plan:
                blocks = []
                for t in range(per):
                    start = pl.multiple_of((row * per + t) * side, side)
                    blocks.append(payloads[group][part][pl.ds(start, side), :])
                b_high, b_low = cut(jnp.concatenate(blocks, axis=1))
                b = jnp.concatenate([b_high, b_low, b_high], axis=0)
                result = lax.dot_general(a, b, TN, preferred_element_type=jnp.float32)
                for t in range(per):
                    target = meta[part, line, lane + t].astype(jnp.int32)
                    place = jnp.minimum(target - first, width)
                    acc[dest, place] += result[:, t * side : (t + 1) * side]
            return 0

        lax.fori_loop(0, count, multiply, 0)
    for row in range(local_rows):
        for t in range(width):
            if base:
                out[row, t] = base[0][row, t] - acc[row, t]
            elif width == slots:
                start = (row * per + t % per) * side
                mine = payloads[t // per][0][start : start + side, :]
                out[row, t] = 2.0 * mine - acc[row, t]
            else:
                start = (row * width + t) * side
                out[start : start + side, :] = acc[row, t]


def shards(density, block_cols, targets):
    local_rows, slots, side, _ = density.shape
    per = slots // 3
    parts = lax.axis_size("inner")
    strip_rows = local_rows * parts
    meta_rows = local_rows * per + -(local_rows * per) % 8
    payload_rows = local_rows * per * side + meta_rows
    anywhere = pl.BlockSpec(memory_space=pl.ANY)
    scalars = pl.BlockSpec(memory_space=pltpu.SMEM)
    vectors = pl.BlockSpec(memory_space=pltpu.VMEM)

    lower, middle, upper = pl.pallas_call(
        functools.partial(pack_kernel, (local_rows, slots, side, strip_rows, meta_rows)),
        out_shape=[jax.ShapeDtypeStruct((payload_rows, side), jnp.float32)] * 3,
        in_specs=[anywhere, vectors, scalars, scalars],
        out_specs=[vectors] * 3,
        scratch_shapes=[pltpu.SemaphoreType.DMA((3, local_rows))],
        compiler_params=pltpu.CompilerParams(vmem_limit_bytes=48 << 20),
        name="pack",
    )(
        density.reshape(-1, side),
        jnp.transpose(targets, (1, 0, 2)),
        block_cols,
        lax.axis_index("inner").reshape(1),
    )

    spare = 32

    def sums(groups, a_at, plan, first, width, offset=0, base=()):
        held = len(groups[0])
        dims = (offset, held, local_rows, slots, side, meta_rows, a_at, len(groups), first, width)
        return pl.pallas_call(
            functools.partial(sums_kernel, dims, plan),
            out_shape=jax.ShapeDtypeStruct(
                (local_rows * per * side + spare, side) if width == per else density.shape,
                jnp.float32,
            ),
            in_specs=[vectors] * (held * len(groups) + len(base)),
            out_specs=vectors,
            scratch_shapes=[
                pltpu.SMEM((held, meta_rows, side), jnp.float32),
                pltpu.SMEM((3, local_rows * per + 1), jnp.int32),
                pltpu.VMEM((local_rows, width + 1, side, side), jnp.float32),
                pltpu.SemaphoreType.DMA((held,)),
            ],
            compiler_params=pltpu.CompilerParams(vmem_limit_bytes=16 << 20),
            cost_estimate=pl.CostEstimate(flops=1, bytes_accessed=1, transcendentals=0),
            name="sums",
        )(*[payload for group in groups for payload in group], *base)

    def spread(far):
        return [one for value in far for one in halves(value)]

    def tied(values, *after):
        return list(lax.optimization_barrier((*values, *after)))[: len(values)]

    own_plan = ((0, 0), (1, per), (2, 2 * per))
    below = shifted(upper, 1)
    lowers, middles, uppers = halves(lower), halves(middle), halves(upper)
    far_lower = across(lower)
    base = sums([lowers, middles, uppers], 1, own_plan, 0, slots)

    far_middle = across(middle, [*far_lower, base])
    far_lowers = spread(tied(far_lower, base))
    far_lowers = tied(far_lowers, below)
    above_own = sums([lowers + far_lowers], 0, ((0, 0),), per, per)
    to_above_own = shifted(above_own, -1)

    far_upper = across(upper, [*far_middle, above_own])
    far_middles = spread(tied(far_middle, above_own))
    all_middles = middles + far_middles
    above_next = sums([lowers + far_lowers, all_middles], 0, ((1, per),), 2 * per, per)
    to_above_next = shifted(above_next, -1)

    belows = halves(below)
    far_below = across(below, [*far_upper, above_next, to_above_own, *belows])
    far_uppers = spread(tied(far_upper, above_next))
    to_next = sums([uppers + far_uppers, all_middles], 0, ((1, per),), 0, per)
    to_below = shifted(to_next, 1)
    if far_lowers:
        near = len(lowers)
        groups = [far_lowers, far_middles, far_uppers]
        base = sums(groups, 1, own_plan, 0, slots, near, [base])
        far_below = tied(far_below, base, to_next, to_above_next)
    belows = belows + spread(far_below)
    from_below = sums([belows], 0, ((0, 2 * per),), per, per)
    ended = tied([to_below, to_above_own, to_above_next, from_below])
    blocks = (local_rows, per, side, side)
    ended = [one[: local_rows * per * side].reshape(blocks) for one in ended]
    received = [ended[0], ended[1] + ended[3], ended[2]]
    return base - jnp.concatenate(received, axis=1)


def solution(mesh):
    return jax.shard_map(
        shards,
        mesh=mesh,
        in_specs=(
            P(("blk", "inner"), None, None, None),
            P(("blk", "inner"), None),
            P(("blk", "inner"), None, None),
        ),
        out_specs=P(("blk", "inner"), None, None, None),
        check_vma=False,
    )
```

```python
import functools

import jax
import jax.numpy as jnp
from jax import lax
from jax.experimental import pallas as pl
from jax.experimental.pallas import tpu as pltpu
from jax.sharding import PartitionSpec as P

TN = (((0,), (0,)), ((), ()))


def shifted(value, steps):
    count = lax.axis_size("blk")
    pairs = [(source, (source + steps) % count) for source in range(count)]
    return lax.ppermute(value, "blk", pairs)


def swapped(value, distance):
    count = lax.axis_size("inner")
    return lax.ppermute(value, "inner", [(i, i ^ distance) for i in range(count)])


def halves(value):
    held = [value]
    for bit in [1 << i for i in range(20) if (1 << i) < lax.axis_size("inner") // 2]:
        held = held + [swapped(one, bit) for one in held]
    return held


def across(value, after=()):
    count = lax.axis_size("inner")
    value = lax.optimization_barrier((value, *after))[0] if after else value
    return [swapped(value, count // 2)] if count > 1 else []


def parted(value, size):
    if size & (size - 1) == 0:
        return value >> (size.bit_length() - 1), value & (size - 1)
    return lax.div(value, size), lax.rem(value, size)


def pack_kernel(dims, density, targets, cols, inner, *refs):
    local_rows, slots, side, strip_rows, meta_rows = dims
    per = slots // 3
    data = local_rows * per * side
    outs, (targets_v, cols_s, sems, meta_sems) = refs[:3], refs[3:]
    arrivals = [
        pltpu.make_async_copy(targets, targets_v, meta_sems.at[0]),
        pltpu.make_async_copy(cols, cols_s, meta_sems.at[1]),
    ]
    for arrival in arrivals:
        arrival.start()
    copies = []
    for group in (0, 2, 1):
        for row in range(local_rows):
            source = density.at[pl.ds((row * slots + group * per) * side, per * side)]
            dest = outs[group].at[pl.ds(row * per * side, per * side)]
            copies.append(pltpu.make_async_copy(source, dest, sems.at[group, row]))
            copies[-1].start()
    for group in (0, 2, 1):
        outs[group][data : data + meta_rows, :] = jnp.zeros((meta_rows, side), jnp.float32)
    for arrival in arrivals:
        arrival.wait()
    for group in (0, 2, 1):
        for row in range(local_rows):
            for slot in range(per):
                in_strip = parted(cols_s[row, group * per + slot], strip_rows)[1]
                owner, line = parted(in_strip, local_rows)
                code = (owner ^ inner[0]) * local_rows + line
                at = data + row * per + slot
                chosen = targets_v[group * per + slot, row : row + 1, :]
                outs[group][at : at + 1, :slots] = chosen.astype(jnp.float32)
                code = jnp.full((1, 1), code, jnp.int32).astype(jnp.float32)
                outs[group][at : at + 1, slots : slots + 1] = code
    for copy in copies:
        copy.wait()


def sums_kernel(dims, plan, *refs):
    offset, parts, local_rows, slots, side, meta_rows, a_at, group_total, first, width = dims
    per = slots // 3
    data = local_rows * per * side
    payloads = [refs[g * parts : (g + 1) * parts] for g in range(group_total)]
    *base, out, meta, listed, acc, meta_sems = refs[group_total * parts :]

    fetches = []
    for part in range(parts):
        source = payloads[a_at][part].at[pl.ds(data, meta_rows)]
        fetches.append(pltpu.make_async_copy(source, meta.at[part], meta_sems.at[part]))
        fetches[-1].start()
    acc[...] = jnp.zeros_like(acc)

    def cut(block):
        high = block.astype(jnp.bfloat16)
        return high, (block - high.astype(jnp.float32)).astype(jnp.bfloat16)

    for part in range(parts):
        fetches[part].wait()
        count = jnp.int32(0)
        for line in range(local_rows * per):
            dest = meta[part, line, slots].astype(jnp.int32) - (offset + part) * local_rows
            listed[0, count] = line
            listed[1, count] = line // per
            listed[2, count] = dest
            mine = (dest >= 0) & (dest < local_rows)
            count = count + mine.astype(jnp.int32)

        def multiply(item, _, part=part):
            line, row, dest = listed[0, item], listed[1, item], listed[2, item]
            start = pl.multiple_of(line * side, side)
            a_high, a_low = cut(payloads[a_at][part][pl.ds(start, side), :])
            a = jnp.concatenate([a_high, a_high, a_low], axis=0)
            for group, lane in plan:
                blocks = []
                for t in range(per):
                    start = pl.multiple_of((row * per + t) * side, side)
                    blocks.append(payloads[group][part][pl.ds(start, side), :])
                b_high, b_low = cut(jnp.concatenate(blocks, axis=1))
                b = jnp.concatenate([b_high, b_low, b_high], axis=0)
                result = lax.dot_general(a, b, TN, preferred_element_type=jnp.float32)
                for t in range(per):
                    target = meta[part, line, lane + t].astype(jnp.int32)
                    place = jnp.minimum(target - first, width)
                    acc[dest, place] += result[:, t * side : (t + 1) * side]
            return 0

        lax.fori_loop(0, count, multiply, 0)
    for row in range(local_rows):
        for t in range(width):
            if base:
                out[row, t] = base[0][row, t] - acc[row, t]
            elif width == slots:
                start = (row * per + t % per) * side
                mine = payloads[t // per][0][start : start + side, :]
                out[row, t] = 2.0 * mine - acc[row, t]
            else:
                start = (row * width + t) * side
                out[start : start + side, :] = acc[row, t]


def finish_kernel(base, to_below, to_above_own, from_below, to_above_next, out, result, sems):
    local_rows, slots, side, _ = base.shape
    per = slots // 3
    copies = []
    for row in range(local_rows):
        for slot in range(per):
            start = (row * per + slot) * side
            lines = slice(start, start + side)
            result[row, slot] = base[row, slot] - to_below[lines, :]
            both = to_above_own[lines, :] + from_below[lines, :]
            result[row, per + slot] = base[row, per + slot] - both
            result[row, 2 * per + slot] = base[row, 2 * per + slot] - to_above_next[lines, :]
        copies.append(pltpu.make_async_copy(result.at[row], out.at[row], sems.at[row]))
        copies[-1].start()
    for copy in copies:
        copy.wait()


def shards(density, block_cols, targets):
    local_rows, slots, side, _ = density.shape
    per = slots // 3
    parts = lax.axis_size("inner")
    strip_rows = local_rows * parts
    meta_rows = local_rows * per + -(local_rows * per) % 8
    used_rows = local_rows * per * side + meta_rows
    payload_rows = used_rows + 16
    in_hbm = pl.BlockSpec(memory_space=pltpu.HBM)
    scalars = pl.BlockSpec(memory_space=pltpu.SMEM)
    vectors = pl.BlockSpec(memory_space=pltpu.VMEM)

    lower, middle, upper = pl.pallas_call(
        functools.partial(pack_kernel, (local_rows, slots, side, strip_rows, meta_rows)),
        out_shape=[jax.ShapeDtypeStruct((payload_rows, side), jnp.float32)] * 3,
        in_specs=[in_hbm, in_hbm, in_hbm, scalars],
        out_specs=[vectors] * 3,
        scratch_shapes=[
            pltpu.VMEM((slots, local_rows, slots), jnp.int32),
            pltpu.SMEM((local_rows, slots), jnp.int32),
            pltpu.SemaphoreType.DMA((3, local_rows)),
            pltpu.SemaphoreType.DMA((2,)),
        ],
        compiler_params=pltpu.CompilerParams(vmem_limit_bytes=48 << 20),
        name="pack",
    )(
        density.reshape(-1, side),
        jnp.transpose(targets, (1, 0, 2)),
        block_cols,
        lax.axis_index("inner").reshape(1),
    )

    spare = 16

    def sums(groups, a_at, plan, first, width, offset=0, base=()):
        held = len(groups[0])
        dims = (offset, held, local_rows, slots, side, meta_rows, a_at, len(groups), first, width)
        return pl.pallas_call(
            functools.partial(sums_kernel, dims, plan),
            out_shape=jax.ShapeDtypeStruct(
                (local_rows * per * side + spare, side) if width == per else density.shape,
                jnp.float32,
            ),
            in_specs=[vectors] * (held * len(groups) + len(base)),
            out_specs=vectors,
            scratch_shapes=[
                pltpu.SMEM((held, meta_rows, side), jnp.float32),
                pltpu.SMEM((3, local_rows * per + 1), jnp.int32),
                pltpu.VMEM((local_rows, width + 1, side, side), jnp.float32),
                pltpu.SemaphoreType.DMA((held,)),
            ],
            compiler_params=pltpu.CompilerParams(vmem_limit_bytes=16 << 20),
            cost_estimate=pl.CostEstimate(flops=1, bytes_accessed=1, transcendentals=0),
            name="sums",
        )(*[payload for group in groups for payload in group], *base)

    def spread(far):
        return [one for value in far for one in halves(value[:used_rows])]

    def tied(values, *after):
        return list(lax.optimization_barrier((*values, *after)))[: len(values)]

    own_plan = ((0, 0), (1, per), (2, 2 * per))
    below = shifted(upper, 1)
    lowers, middles, uppers = halves(lower), halves(middle), halves(upper)
    far_lower = across(lower)
    base = sums([lowers, middles, uppers], 1, own_plan, 0, slots)

    far_middle = across(middle, [base])
    far_lowers = spread(tied(far_lower, base))
    far_lowers = tied(far_lowers, below)
    above_own = sums([lowers + far_lowers], 0, ((0, 0),), per, per)
    to_above_own = shifted(above_own, -1)

    far_upper = across(upper, [above_own])
    far_middles = spread(tied(far_middle, above_own))
    all_middles = middles + far_middles
    above_next = sums([lowers + far_lowers, all_middles], 0, ((1, per),), 2 * per, per)
    to_above_next = shifted(above_next, -1)

    belows = halves(below)
    far_below = across(below, [above_next, to_above_own, *belows])
    far_uppers = spread(tied(far_upper, above_next))
    to_next = sums([uppers + far_uppers, all_middles], 0, ((1, per),), 0, per)
    to_below = shifted(to_next, 1)
    if far_lowers:
        near = len(lowers)
        groups = [far_lowers, far_middles, far_uppers]
        base = sums(groups, 1, own_plan, 0, slots, near, [base])
        far_below = tied(far_below, base, to_next, to_above_next)
    belows = belows + spread(far_below)
    from_below = sums([belows], 0, ((0, 2 * per),), per, per)
    return pl.pallas_call(
        finish_kernel,
        out_shape=jax.ShapeDtypeStruct(density.shape, jnp.float32),
        in_specs=[vectors] * 5,
        out_specs=in_hbm,
        scratch_shapes=[
            pltpu.VMEM(density.shape, jnp.float32),
            pltpu.SemaphoreType.DMA((local_rows,)),
        ],
        compiler_params=pltpu.CompilerParams(vmem_limit_bytes=16 << 20),
        cost_estimate=pl.CostEstimate(flops=1, bytes_accessed=1, transcendentals=0),
        name="finish",
    )(base, to_below, to_above_own, from_below, to_above_next)


def solution(mesh):
    return jax.shard_map(
        shards,
        mesh=mesh,
        in_specs=(
            P(("blk", "inner"), None, None, None),
            P(("blk", "inner"), None),
            P(("blk", "inner"), None, None),
        ),
        out_specs=P(("blk", "inner"), None, None, None),
        check_vma=False,
    )
```

```python
import functools

import jax
import jax.numpy as jnp
from jax import lax
from jax.experimental import pallas as pl
from jax.experimental.pallas import tpu as pltpu
from jax.sharding import PartitionSpec as P

TN = (((0,), (0,)), ((), ()))


def shifted(value, steps):
    count = lax.axis_size("blk")
    pairs = [(source, (source + steps) % count) for source in range(count)]
    return lax.ppermute(value, "blk", pairs)


def swapped(value, distance):
    count = lax.axis_size("inner")
    return lax.ppermute(value, "inner", [(i, i ^ distance) for i in range(count)])


def halves(value):
    held = [value]
    for bit in [1 << i for i in range(20) if (1 << i) < lax.axis_size("inner") // 2]:
        held = held + [swapped(one, bit) for one in held]
    return held


def across(value, after=()):
    count = lax.axis_size("inner")
    value = lax.optimization_barrier((value, *after))[0] if after else value
    return [swapped(value, count // 2)] if count > 1 else []


def parted(value, size):
    if size & (size - 1) == 0:
        return value >> (size.bit_length() - 1), value & (size - 1)
    return lax.div(value, size), lax.rem(value, size)


def pack_kernel(dims, density, targets, cols, inner, *refs):
    local_rows, slots, side, strip_rows, meta_rows = dims
    per = slots // 3
    data = local_rows * per * side
    outs, (targets_v, cols_s, sems, meta_sems) = refs[:3], refs[3:]
    arrivals = [
        pltpu.make_async_copy(targets, targets_v, meta_sems.at[0]),
        pltpu.make_async_copy(cols, cols_s, meta_sems.at[1]),
    ]
    for arrival in arrivals:
        arrival.start()
    copies = []
    for group in (0, 2, 1):
        for row in range(local_rows):
            source = density.at[pl.ds((row * slots + group * per) * side, per * side)]
            dest = outs[group].at[pl.ds(row * per * side, per * side)]
            copies.append(pltpu.make_async_copy(source, dest, sems.at[group, row]))
            copies[-1].start()
    for group in (0, 2, 1):
        outs[group][data : data + meta_rows, :] = jnp.zeros((meta_rows, side), jnp.float32)
    for arrival in arrivals:
        arrival.wait()
    for group in (0, 2, 1):
        for row in range(local_rows):
            for slot in range(per):
                in_strip = parted(cols_s[row, group * per + slot], strip_rows)[1]
                owner, line = parted(in_strip, local_rows)
                code = (owner ^ inner[0]) * local_rows + line
                at = data + row * per + slot
                chosen = targets_v[group * per + slot, row : row + 1, :]
                outs[group][at : at + 1, :slots] = chosen.astype(jnp.float32)
                code = jnp.full((1, 1), code, jnp.int32).astype(jnp.float32)
                outs[group][at : at + 1, slots : slots + 1] = code
    for copy in copies:
        copy.wait()


def sums_kernel(dims, plan, *refs):
    offset, parts, local_rows, slots, side, meta_rows, a_at, group_total, first, width = dims
    per = slots // 3
    data = local_rows * per * side
    payloads = [refs[g * parts : (g + 1) * parts] for g in range(group_total)]
    *base, out, meta, listed, acc, meta_sems = refs[group_total * parts :]

    fetches = []
    for part in range(parts):
        source = payloads[a_at][part].at[pl.ds(data, meta_rows)]
        fetches.append(pltpu.make_async_copy(source, meta.at[part], meta_sems.at[part]))
        fetches[-1].start()
    acc[...] = jnp.zeros_like(acc)

    def cut(block):
        high = block.astype(jnp.bfloat16)
        return high, (block - high.astype(jnp.float32)).astype(jnp.bfloat16)

    for part in range(parts):
        fetches[part].wait()
        count = jnp.int32(0)
        for line in range(local_rows * per):
            dest = meta[part, line, slots].astype(jnp.int32) - (offset + part) * local_rows
            listed[0, count] = line
            listed[1, count] = line // per
            listed[2, count] = dest
            mine = (dest >= 0) & (dest < local_rows)
            count = count + mine.astype(jnp.int32)

        def multiply(item, _, part=part):
            line, row, dest = listed[0, item], listed[1, item], listed[2, item]
            start = pl.multiple_of(line * side, side)
            a_high, a_low = cut(payloads[a_at][part][pl.ds(start, side), :])
            a = jnp.concatenate([a_high, a_high, a_low], axis=0)
            for group, lane in plan:
                blocks = []
                for t in range(per):
                    start = pl.multiple_of((row * per + t) * side, side)
                    blocks.append(payloads[group][part][pl.ds(start, side), :])
                b_high, b_low = cut(jnp.concatenate(blocks, axis=1))
                b = jnp.concatenate([b_high, b_low, b_high], axis=0)
                result = lax.dot_general(a, b, TN, preferred_element_type=jnp.float32)
                for t in range(per):
                    target = meta[part, line, lane + t].astype(jnp.int32)
                    place = jnp.minimum(target - first, width)
                    acc[dest, place] += result[:, t * side : (t + 1) * side]
            return 0

        lax.fori_loop(0, count, multiply, 0)
    for row in range(local_rows):
        for t in range(width):
            if base:
                out[row, t] = base[0][row, t] - acc[row, t]
            elif width == slots:
                start = (row * per + t % per) * side
                mine = payloads[t // per][0][start : start + side, :]
                out[row, t] = 2.0 * mine - acc[row, t]
            else:
                start = (row * width + t) * side
                out[start : start + side, :] = acc[row, t]


def finish_kernel(base, to_below, to_above_own, from_below, to_above_next, out, result, sems):
    local_rows, slots, side, _ = base.shape
    per = slots // 3
    copies = []
    for row in range(local_rows):
        for slot in range(per):
            start = (row * per + slot) * side
            lines = slice(start, start + side)
            result[row, slot] = base[row, slot] - to_below[lines, :]
            both = to_above_own[lines, :] + from_below[lines, :]
            result[row, per + slot] = base[row, per + slot] - both
            result[row, 2 * per + slot] = base[row, 2 * per + slot] - to_above_next[lines, :]
        copies.append(pltpu.make_async_copy(result.at[row], out.at[row], sems.at[row]))
        copies[-1].start()
    for copy in copies:
        copy.wait()


def shards(density, block_cols, targets):
    local_rows, slots, side, _ = density.shape
    per = slots // 3
    parts = lax.axis_size("inner")
    strip_rows = local_rows * parts
    meta_rows = local_rows * per + -(local_rows * per) % 8
    used_rows = local_rows * per * side + meta_rows
    payload_rows = used_rows + 24
    in_hbm = pl.BlockSpec(memory_space=pltpu.HBM)
    scalars = pl.BlockSpec(memory_space=pltpu.SMEM)
    vectors = pl.BlockSpec(memory_space=pltpu.VMEM)

    lower, middle, upper = pl.pallas_call(
        functools.partial(pack_kernel, (local_rows, slots, side, strip_rows, meta_rows)),
        out_shape=[jax.ShapeDtypeStruct((payload_rows, side), jnp.float32)] * 3,
        in_specs=[in_hbm, in_hbm, in_hbm, scalars],
        out_specs=[vectors] * 3,
        scratch_shapes=[
            pltpu.VMEM((slots, local_rows, slots), jnp.int32),
            pltpu.SMEM((local_rows, slots), jnp.int32),
            pltpu.SemaphoreType.DMA((3, local_rows)),
            pltpu.SemaphoreType.DMA((2,)),
        ],
        compiler_params=pltpu.CompilerParams(vmem_limit_bytes=52 << 20),
        name="pack",
    )(
        density.reshape(-1, side),
        jnp.transpose(targets, (1, 0, 2)),
        block_cols,
        lax.axis_index("inner").reshape(1),
    )

    spare = 24

    def sums(groups, a_at, plan, first, width, offset=0, base=()):
        held = len(groups[0])
        dims = (offset, held, local_rows, slots, side, meta_rows, a_at, len(groups), first, width)
        return pl.pallas_call(
            functools.partial(sums_kernel, dims, plan),
            out_shape=jax.ShapeDtypeStruct(
                (local_rows * per * side + spare, side) if width == per else density.shape,
                jnp.float32,
            ),
            in_specs=[vectors] * (held * len(groups) + len(base)),
            out_specs=vectors,
            scratch_shapes=[
                pltpu.SMEM((held, meta_rows, side), jnp.float32),
                pltpu.SMEM((3, local_rows * per + 1), jnp.int32),
                pltpu.VMEM((local_rows, width + 1, side, side), jnp.float32),
                pltpu.SemaphoreType.DMA((held,)),
            ],
            compiler_params=pltpu.CompilerParams(vmem_limit_bytes=16 << 20),
            cost_estimate=pl.CostEstimate(flops=1, bytes_accessed=1, transcendentals=0),
            name="sums",
        )(*[payload for group in groups for payload in group], *base)

    def spread(far):
        return [one for value in far for one in halves(value[:used_rows])]

    def tied(values, *after):
        return list(lax.optimization_barrier((*values, *after)))[: len(values)]

    own_plan = ((0, 0), (1, per), (2, 2 * per))
    below = shifted(upper, 1)
    lowers, middles, uppers = halves(lower), halves(middle), halves(upper)
    far_lower = across(lower)
    base = sums([lowers, middles, uppers], 1, own_plan, 0, slots)

    far_middle = across(middle, [base])
    far_lowers = spread(tied(far_lower, base))
    far_lowers = tied(far_lowers, below)
    above_own = sums([lowers + far_lowers], 0, ((0, 0),), per, per)
    to_above_own = shifted(above_own, -1)

    far_upper = across(upper, [above_own])
    far_middles = spread(tied(far_middle, above_own))
    all_middles = middles + far_middles
    above_next = sums([lowers + far_lowers, all_middles], 0, ((1, per),), 2 * per, per)
    to_above_next = shifted(above_next, -1)

    belows = halves(below)
    far_below = across(below, [above_next, *belows])
    far_uppers = spread(tied(far_upper, above_next, to_above_own))
    to_next = sums([uppers + far_uppers, all_middles], 0, ((1, per),), 0, per)
    to_below = shifted(to_next, 1)
    if far_lowers:
        near = len(lowers)
        groups = [far_lowers, far_middles, far_uppers]
        base = sums(groups, 1, own_plan, 0, slots, near, [base])
        far_below = tied(far_below, base, to_next, to_above_next)
    belows = belows + spread(far_below)
    from_below = sums([belows], 0, ((0, 2 * per),), per, per)
    return pl.pallas_call(
        finish_kernel,
        out_shape=jax.ShapeDtypeStruct(density.shape, jnp.float32),
        in_specs=[vectors] * 5,
        out_specs=in_hbm,
        scratch_shapes=[
            pltpu.VMEM(density.shape, jnp.float32),
            pltpu.SemaphoreType.DMA((local_rows,)),
        ],
        compiler_params=pltpu.CompilerParams(vmem_limit_bytes=16 << 20),
        cost_estimate=pl.CostEstimate(flops=1, bytes_accessed=1, transcendentals=0),
        name="finish",
    )(base, to_below, to_above_own, from_below, to_above_next)


def solution(mesh):
    return jax.shard_map(
        shards,
        mesh=mesh,
        in_specs=(
            P(("blk", "inner"), None, None, None),
            P(("blk", "inner"), None),
            P(("blk", "inner"), None, None),
        ),
        out_specs=P(("blk", "inner"), None, None, None),
        check_vma=False,
    )
```

```python
import functools

import jax
import jax.numpy as jnp
from jax import lax
from jax.experimental import pallas as pl
from jax.experimental.pallas import tpu as pltpu
from jax.sharding import PartitionSpec as P

TN = (((0,), (0,)), ((), ()))


def shifted(value, steps):
    count = lax.axis_size("blk")
    pairs = [(source, (source + steps) % count) for source in range(count)]
    return lax.ppermute(value, "blk", pairs)


def swapped(value, distance):
    count = lax.axis_size("inner")
    return lax.ppermute(value, "inner", [(i, i ^ distance) for i in range(count)])


def halves(value):
    held = [value]
    for bit in [1 << i for i in range(20) if (1 << i) < lax.axis_size("inner") // 2]:
        held = held + [swapped(one, bit) for one in held]
    return held


def across(value, after=()):
    count = lax.axis_size("inner")
    value = lax.optimization_barrier((value, *after))[0] if after else value
    return [swapped(value, count // 2)] if count > 1 else []


def parted(value, size):
    if size & (size - 1) == 0:
        return value >> (size.bit_length() - 1), value & (size - 1)
    return lax.div(value, size), lax.rem(value, size)


def pack_kernel(dims, density, targets, cols, inner, *refs):
    local_rows, slots, side, strip_rows, meta_rows = dims
    per = slots // 3
    data = local_rows * per * side
    outs, (targets_v, cols_s, sems, meta_sems) = refs[:3], refs[3:]
    arrivals = [
        pltpu.make_async_copy(targets, targets_v, meta_sems.at[0]),
        pltpu.make_async_copy(cols, cols_s, meta_sems.at[1]),
    ]
    for arrival in arrivals:
        arrival.start()
    copies = []
    for group in (0, 2, 1):
        for row in range(local_rows):
            source = density.at[pl.ds((row * slots + group * per) * side, per * side)]
            dest = outs[group].at[pl.ds(row * per * side, per * side)]
            copies.append(pltpu.make_async_copy(source, dest, sems.at[group, row]))
            copies[-1].start()
    for group in (0, 2, 1):
        outs[group][data : data + meta_rows, :] = jnp.zeros((meta_rows, side), jnp.float32)
    for arrival in arrivals:
        arrival.wait()
    for group in (0, 2, 1):
        for row in range(local_rows):
            for slot in range(per):
                in_strip = parted(cols_s[row, group * per + slot], strip_rows)[1]
                owner, line = parted(in_strip, local_rows)
                code = (owner ^ inner[0]) * local_rows + line
                at = data + row * per + slot
                chosen = targets_v[group * per + slot, row : row + 1, :]
                outs[group][at : at + 1, :slots] = chosen.astype(jnp.float32)
                code = jnp.full((1, 1), code, jnp.int32).astype(jnp.float32)
                outs[group][at : at + 1, slots : slots + 1] = code
    for copy in copies:
        copy.wait()


def sums_kernel(dims, plan, *refs):
    offset, parts, local_rows, slots, side, meta_rows, a_at, group_total, first, width = dims
    per = slots // 3
    data = local_rows * per * side
    payloads = [refs[g * parts : (g + 1) * parts] for g in range(group_total)]
    *base, out, meta, listed, acc, meta_sems = refs[group_total * parts :]

    fetches = []
    for part in range(parts):
        source = payloads[a_at][part].at[pl.ds(data, meta_rows)]
        fetches.append(pltpu.make_async_copy(source, meta.at[part], meta_sems.at[part]))
        fetches[-1].start()
    acc[...] = jnp.zeros_like(acc)

    def cut(block):
        high = block.astype(jnp.bfloat16)
        return high, (block - high.astype(jnp.float32)).astype(jnp.bfloat16)

    for part in range(parts):
        fetches[part].wait()
        count = jnp.int32(0)
        for line in range(local_rows * per):
            dest = meta[part, line, slots].astype(jnp.int32) - (offset + part) * local_rows
            listed[0, count] = line
            listed[1, count] = line // per
            listed[2, count] = dest
            mine = (dest >= 0) & (dest < local_rows)
            count = count + mine.astype(jnp.int32)

        def multiply(item, _, part=part):
            line, row, dest = listed[0, item], listed[1, item], listed[2, item]
            start = pl.multiple_of(line * side, side)
            a_high, a_low = cut(payloads[a_at][part][pl.ds(start, side), :])
            a = jnp.concatenate([a_high, a_high, a_low], axis=0)
            for group, lane in plan:
                blocks = []
                for t in range(per):
                    start = pl.multiple_of((row * per + t) * side, side)
                    blocks.append(payloads[group][part][pl.ds(start, side), :])
                b_high, b_low = cut(jnp.concatenate(blocks, axis=1))
                b = jnp.concatenate([b_high, b_low, b_high], axis=0)
                result = lax.dot_general(a, b, TN, preferred_element_type=jnp.float32)
                for t in range(per):
                    target = meta[part, line, lane + t].astype(jnp.int32)
                    place = jnp.minimum(target - first, width)
                    acc[dest, place] += result[:, t * side : (t + 1) * side]
            return 0

        lax.fori_loop(0, count, multiply, 0)
    for row in range(local_rows):
        for t in range(width):
            if base:
                out[row, t] = base[0][row, t] - acc[row, t]
            elif width == slots:
                start = (row * per + t % per) * side
                mine = payloads[t // per][0][start : start + side, :]
                out[row, t] = 2.0 * mine - acc[row, t]
            else:
                start = (row * width + t) * side
                out[start : start + side, :] = acc[row, t]


def finish_kernel(base, to_below, to_above_own, from_below, to_above_next, out, result, sems):
    local_rows, slots, side, _ = base.shape
    per = slots // 3
    copies = []
    for row in range(local_rows):
        for slot in range(per):
            start = (row * per + slot) * side
            lines = slice(start, start + side)
            result[row, slot] = base[row, slot] - to_below[lines, :]
            both = to_above_own[lines, :] + from_below[lines, :]
            result[row, per + slot] = base[row, per + slot] - both
            result[row, 2 * per + slot] = base[row, 2 * per + slot] - to_above_next[lines, :]
        copies.append(pltpu.make_async_copy(result.at[row], out.at[row], sems.at[row]))
        copies[-1].start()
    for copy in copies:
        copy.wait()


def shards(density, block_cols, targets):
    local_rows, slots, side, _ = density.shape
    per = slots // 3
    parts = lax.axis_size("inner")
    strip_rows = local_rows * parts
    meta_rows = local_rows * per + -(local_rows * per) % 8
    used_rows = local_rows * per * side + meta_rows
    payload_rows = used_rows + 2
    in_hbm = pl.BlockSpec(memory_space=pltpu.HBM)
    scalars = pl.BlockSpec(memory_space=pltpu.SMEM)
    vectors = pl.BlockSpec(memory_space=pltpu.VMEM)

    lower, middle, upper = pl.pallas_call(
        functools.partial(pack_kernel, (local_rows, slots, side, strip_rows, meta_rows)),
        out_shape=[jax.ShapeDtypeStruct((payload_rows, side), jnp.float32)] * 3,
        in_specs=[in_hbm, in_hbm, in_hbm, scalars],
        out_specs=[vectors] * 3,
        scratch_shapes=[
            pltpu.VMEM((slots, local_rows, slots), jnp.int32),
            pltpu.SMEM((local_rows, slots), jnp.int32),
            pltpu.SemaphoreType.DMA((3, local_rows)),
            pltpu.SemaphoreType.DMA((2,)),
        ],
        compiler_params=pltpu.CompilerParams(vmem_limit_bytes=52 << 20),
        name="pack",
    )(
        density.reshape(-1, side),
        jnp.transpose(targets, (1, 0, 2)),
        block_cols,
        lax.axis_index("inner").reshape(1),
    )

    spare = 11

    def sums(groups, a_at, plan, first, width, offset=0, base=()):
        held = len(groups[0])
        dims = (offset, held, local_rows, slots, side, meta_rows, a_at, len(groups), first, width)
        return pl.pallas_call(
            functools.partial(sums_kernel, dims, plan),
            out_shape=jax.ShapeDtypeStruct(
                (local_rows * per * side + spare, side) if width == per else density.shape,
                jnp.float32,
            ),
            in_specs=[vectors] * (held * len(groups) + len(base)),
            out_specs=vectors,
            scratch_shapes=[
                pltpu.SMEM((held, meta_rows, side), jnp.float32),
                pltpu.SMEM((3, local_rows * per + 1), jnp.int32),
                pltpu.VMEM((local_rows, width + 1, side, side), jnp.float32),
                pltpu.SemaphoreType.DMA((held,)),
            ],
            compiler_params=pltpu.CompilerParams(vmem_limit_bytes=16 << 20),
            cost_estimate=pl.CostEstimate(flops=1, bytes_accessed=1, transcendentals=0),
            name="sums",
        )(*[payload for group in groups for payload in group], *base)

    def spread(far):
        return [one for value in far for one in halves(value[:used_rows])]

    def tied(values, *after):
        return list(lax.optimization_barrier((*values, *after)))[: len(values)]

    own_plan = ((0, 0), (1, per), (2, 2 * per))
    below = shifted(upper, 1)
    lowers, middles, uppers = halves(lower), halves(middle), halves(upper)
    far_lower = across(lower)
    base = sums([lowers, middles, uppers], 1, own_plan, 0, slots)

    far_middle = across(middle, [*far_lower, base])
    far_lowers = spread(tied(far_lower, base))
    far_lowers = tied(far_lowers, below)
    above_own = sums([lowers + far_lowers], 0, ((0, 0),), per, per)
    to_above_own = shifted(above_own, -1)

    far_upper = across(upper, [*far_middle, above_own])
    far_middles = spread(tied(far_middle, above_own))
    all_middles = middles + far_middles
    above_next = sums([lowers + far_lowers, all_middles], 0, ((1, per),), 2 * per, per)
    to_above_next = shifted(above_next, -1)

    belows = halves(below)
    far_below = across(below, [*far_upper, above_next, *belows])
    far_uppers = spread(tied(far_upper, above_next, to_above_own))
    to_next = sums([uppers + far_uppers, all_middles], 0, ((1, per),), 0, per)
    to_below = shifted(to_next, 1)
    if far_lowers:
        near = len(lowers)
        groups = [far_lowers, far_middles, far_uppers]
        base = sums(groups, 1, own_plan, 0, slots, near, [base])
        far_below = tied(far_below, base, to_next, to_above_next)
    belows = belows + spread(far_below)
    from_below = sums([belows], 0, ((0, 2 * per),), per, per)
    return pl.pallas_call(
        finish_kernel,
        out_shape=jax.ShapeDtypeStruct(density.shape, jnp.float32),
        in_specs=[vectors] * 5,
        out_specs=in_hbm,
        scratch_shapes=[
            pltpu.VMEM(density.shape, jnp.float32),
            pltpu.SemaphoreType.DMA((local_rows,)),
        ],
        compiler_params=pltpu.CompilerParams(vmem_limit_bytes=16 << 20),
        cost_estimate=pl.CostEstimate(flops=1, bytes_accessed=1, transcendentals=0),
        name="finish",
    )(base, to_below, to_above_own, from_below, to_above_next)


def solution(mesh):
    return jax.shard_map(
        shards,
        mesh=mesh,
        in_specs=(
            P(("blk", "inner"), None, None, None),
            P(("blk", "inner"), None),
            P(("blk", "inner"), None, None),
        ),
        out_specs=P(("blk", "inner"), None, None, None),
        check_vma=False,
    )
```

```python
import functools

import jax
import jax.numpy as jnp
from jax import lax
from jax.experimental import pallas as pl
from jax.experimental.pallas import tpu as pltpu
from jax.sharding import PartitionSpec as P

TN = (((0,), (0,)), ((), ()))


def shifted(value, steps):
    count = lax.axis_size("blk")
    pairs = [(source, (source + steps) % count) for source in range(count)]
    return lax.ppermute(value, "blk", pairs)


def swapped(value, distance):
    count = lax.axis_size("inner")
    return lax.ppermute(value, "inner", [(i, i ^ distance) for i in range(count)])


def halves(value):
    held = [value]
    for bit in [1 << i for i in range(20) if (1 << i) < lax.axis_size("inner") // 2]:
        held = held + [swapped(one, bit) for one in held]
    return held


def across(value, after=()):
    count = lax.axis_size("inner")
    value = lax.optimization_barrier((value, *after))[0] if after else value
    return [swapped(value, count // 2)] if count > 1 else []


def parted(value, size):
    if size & (size - 1) == 0:
        return value >> (size.bit_length() - 1), value & (size - 1)
    return lax.div(value, size), lax.rem(value, size)


def pack_kernel(dims, density, targets, cols, inner, *refs):
    local_rows, slots, side, strip_rows, meta_rows = dims
    per = slots // 3
    data = local_rows * per * side
    outs, (targets_v, cols_s, sems, meta_sems) = refs[:3], refs[3:]
    arrivals = [
        pltpu.make_async_copy(targets, targets_v, meta_sems.at[0]),
        pltpu.make_async_copy(cols, cols_s, meta_sems.at[1]),
    ]
    for arrival in arrivals:
        arrival.start()
    copies = []
    for group in (0, 2, 1):
        for row in range(local_rows):
            source = density.at[pl.ds((row * slots + group * per) * side, per * side)]
            dest = outs[group].at[pl.ds(row * per * side, per * side)]
            copies.append(pltpu.make_async_copy(source, dest, sems.at[group, row]))
            copies[-1].start()
    for group in (0, 2, 1):
        outs[group][data : data + meta_rows, :] = jnp.zeros((meta_rows, side), jnp.float32)
    for arrival in arrivals:
        arrival.wait()
    for group in (0, 2, 1):
        for row in range(local_rows):
            for slot in range(per):
                in_strip = parted(cols_s[row, group * per + slot], strip_rows)[1]
                owner, line = parted(in_strip, local_rows)
                code = (owner ^ inner[0]) * local_rows + line
                at = data + row * per + slot
                chosen = targets_v[group * per + slot, row : row + 1, :]
                outs[group][at : at + 1, :slots] = chosen.astype(jnp.float32)
                code = jnp.full((1, 1), code, jnp.int32).astype(jnp.float32)
                outs[group][at : at + 1, slots : slots + 1] = code
    for copy in copies:
        copy.wait()


def sums_kernel(dims, plan, *refs):
    offset, parts, local_rows, slots, side, meta_rows, a_at, group_total, first, width = dims
    per = slots // 3
    data = local_rows * per * side
    payloads = [refs[g * parts : (g + 1) * parts] for g in range(group_total)]
    *base, out, meta, listed, acc, meta_sems = refs[group_total * parts :]

    fetches = []
    for part in range(parts):
        source = payloads[a_at][part].at[pl.ds(data, meta_rows)]
        fetches.append(pltpu.make_async_copy(source, meta.at[part], meta_sems.at[part]))
        fetches[-1].start()
    acc[...] = jnp.zeros_like(acc)

    def cut(block):
        high = block.astype(jnp.bfloat16)
        return high, (block - high.astype(jnp.float32)).astype(jnp.bfloat16)

    for part in range(parts):
        fetches[part].wait()
        count = jnp.int32(0)
        for line in range(local_rows * per):
            dest = meta[part, line, slots].astype(jnp.int32) - (offset + part) * local_rows
            listed[0, count] = line
            listed[1, count] = line // per
            listed[2, count] = dest
            mine = (dest >= 0) & (dest < local_rows)
            count = count + mine.astype(jnp.int32)

        def multiply(item, _, part=part):
            line, row, dest = listed[0, item], listed[1, item], listed[2, item]
            start = pl.multiple_of(line * side, side)
            a_high, a_low = cut(payloads[a_at][part][pl.ds(start, side), :])
            a = jnp.concatenate([a_high, a_high, a_low], axis=0)
            for group, lane in plan:
                blocks = []
                for t in range(per):
                    start = pl.multiple_of((row * per + t) * side, side)
                    blocks.append(payloads[group][part][pl.ds(start, side), :])
                b_high, b_low = cut(jnp.concatenate(blocks, axis=1))
                b = jnp.concatenate([b_high, b_low, b_high], axis=0)
                result = lax.dot_general(a, b, TN, preferred_element_type=jnp.float32)
                for t in range(per):
                    target = meta[part, line, lane + t].astype(jnp.int32)
                    place = jnp.minimum(target - first, width)
                    acc[dest, place] += result[:, t * side : (t + 1) * side]
            return 0

        lax.fori_loop(0, count, multiply, 0)
    for row in range(local_rows):
        for t in range(width):
            if base:
                out[row, t] = base[0][row, t] - acc[row, t]
            elif width == slots:
                start = (row * per + t % per) * side
                mine = payloads[t // per][0][start : start + side, :]
                out[row, t] = 2.0 * mine - acc[row, t]
            else:
                start = (row * width + t) * side
                out[start : start + side, :] = acc[row, t]


def finish_kernel(base, lower, middle, own_middle, upper, out, result, sems):
    local_rows, slots, side, _ = base.shape
    per = slots // 3
    copies = []
    for row in range(local_rows):
        for slot in range(per):
            start = (row * per + slot) * side
            lines = slice(start, start + side)
            result[row, slot] = base[row, slot] - lower[lines, :]
            both = middle[lines, :] + own_middle[lines, :]
            result[row, per + slot] = base[row, per + slot] - both
            result[row, 2 * per + slot] = base[row, 2 * per + slot] - upper[lines, :]
        copies.append(pltpu.make_async_copy(result.at[row], out.at[row], sems.at[row]))
        copies[-1].start()
    for copy in copies:
        copy.wait()


def shards(density, block_cols, targets):
    local_rows, slots, side, _ = density.shape
    per = slots // 3
    parts = lax.axis_size("inner")
    strip_rows = local_rows * parts
    meta_rows = local_rows * per + -(local_rows * per) % 8
    used_rows = local_rows * per * side + meta_rows
    payload_rows = used_rows + 3
    in_hbm = pl.BlockSpec(memory_space=pltpu.HBM)
    scalars = pl.BlockSpec(memory_space=pltpu.SMEM)
    vectors = pl.BlockSpec(memory_space=pltpu.VMEM)

    lower, middle, upper = pl.pallas_call(
        functools.partial(pack_kernel, (local_rows, slots, side, strip_rows, meta_rows)),
        out_shape=[jax.ShapeDtypeStruct((payload_rows, side), jnp.float32)] * 3,
        in_specs=[in_hbm, in_hbm, in_hbm, scalars],
        out_specs=[vectors] * 3,
        scratch_shapes=[
            pltpu.VMEM((slots, local_rows, slots), jnp.int32),
            pltpu.SMEM((local_rows, slots), jnp.int32),
            pltpu.SemaphoreType.DMA((3, local_rows)),
            pltpu.SemaphoreType.DMA((2,)),
        ],
        compiler_params=pltpu.CompilerParams(vmem_limit_bytes=52 << 20),
        name="pack",
    )(
        density.reshape(-1, side),
        jnp.transpose(targets, (1, 0, 2)),
        block_cols,
        lax.axis_index("inner").reshape(1),
    )

    spare = 10

    def sums(groups, a_at, plan, first, width, offset=0, base=()):
        held = len(groups[0])
        dims = (offset, held, local_rows, slots, side, meta_rows, a_at, len(groups), first, width)
        return pl.pallas_call(
            functools.partial(sums_kernel, dims, plan),
            out_shape=jax.ShapeDtypeStruct(
                (local_rows * per * side + spare, side) if width == per else density.shape,
                jnp.float32,
            ),
            in_specs=[vectors] * (held * len(groups) + len(base)),
            out_specs=vectors,
            scratch_shapes=[
                pltpu.SMEM((held, meta_rows, side), jnp.float32),
                pltpu.SMEM((3, local_rows * per + 1), jnp.int32),
                pltpu.VMEM((local_rows, width + 1, side, side), jnp.float32),
                pltpu.SemaphoreType.DMA((held,)),
            ],
            compiler_params=pltpu.CompilerParams(vmem_limit_bytes=16 << 20),
            cost_estimate=pl.CostEstimate(flops=1, bytes_accessed=1, transcendentals=0),
            name="sums",
        )(*[payload for group in groups for payload in group], *base)

    def spread(far):
        return [one for value in far for one in halves(value[:used_rows])]

    def tied(values, *after):
        return list(lax.optimization_barrier((*values, *after)))[: len(values)]

    own_plan = ((0, 0), (1, per), (2, 2 * per))
    above = shifted(lower, -1)
    lowers, middles, uppers = halves(lower), halves(middle), halves(upper)
    far_upper = across(upper)
    base = sums([lowers, middles, uppers], 1, own_plan, 0, slots)

    far_middle = across(middle, [base])
    far_uppers = tied(spread(far_upper), above) if far_upper else []
    below_own = sums([uppers + far_uppers], 0, ((0, 2 * per),), per, per)

    far_lower = across(lower, [below_own])
    to_below_own = shifted(below_own, 1)
    far_middles = spread(tied(far_middle, below_own))
    all_middles = middles + far_middles
    below_next = sums([uppers + far_uppers, all_middles], 0, ((1, per),), 0, per)

    aboves = halves(above)
    far_above = across(above, [below_next, *aboves])
    to_below_next = shifted(below_next, 1)
    far_lowers = spread(tied(far_lower, below_next, to_below_own))
    above_next = sums([lowers + far_lowers, all_middles], 0, ((1, per),), 2 * per, per)
    to_above_next = shifted(above_next, -1)
    if far_lowers:
        near = len(lowers)
        groups = [far_lowers, far_middles, far_uppers]
        base = sums(groups, 1, own_plan, 0, slots, near, [base])
        far_above = tied(far_above, base, above_next, to_below_next)
    aboves = aboves + spread(far_above)
    from_above = sums([aboves], 0, ((0, 0),), per, per)
    return pl.pallas_call(
        finish_kernel,
        out_shape=jax.ShapeDtypeStruct(density.shape, jnp.float32),
        in_specs=[vectors] * 5,
        out_specs=in_hbm,
        scratch_shapes=[
            pltpu.VMEM(density.shape, jnp.float32),
            pltpu.SemaphoreType.DMA((local_rows,)),
        ],
        compiler_params=pltpu.CompilerParams(vmem_limit_bytes=16 << 20),
        cost_estimate=pl.CostEstimate(flops=1, bytes_accessed=1, transcendentals=0),
        name="finish",
    )(base, to_below_next, to_below_own, from_above, to_above_next)


def solution(mesh):
    return jax.shard_map(
        shards,
        mesh=mesh,
        in_specs=(
            P(("blk", "inner"), None, None, None),
            P(("blk", "inner"), None),
            P(("blk", "inner"), None, None),
        ),
        out_specs=P(("blk", "inner"), None, None, None),
        check_vma=False,
    )
```

```python
import functools

import jax
import jax.numpy as jnp
from jax import lax
from jax.experimental import pallas as pl
from jax.experimental.pallas import tpu as pltpu
from jax.sharding import PartitionSpec as P

TN = (((0,), (0,)), ((), ()))


def shifted(value, steps):
    count = lax.axis_size("blk")
    pairs = [(source, (source + steps) % count) for source in range(count)]
    return lax.ppermute(value, "blk", pairs)


def swapped(value, distance):
    count = lax.axis_size("inner")
    return lax.ppermute(value, "inner", [(i, i ^ distance) for i in range(count)])


def halves(value):
    held = [value]
    for bit in [1 << i for i in range(20) if (1 << i) < lax.axis_size("inner") // 2]:
        held = held + [swapped(one, bit) for one in held]
    return held


def across(value, after=()):
    count = lax.axis_size("inner")
    value = lax.optimization_barrier((value, *after))[0] if after else value
    return [swapped(value, count // 2)] if count > 1 else []


def parted(value, size):
    if size & (size - 1) == 0:
        return value >> (size.bit_length() - 1), value & (size - 1)
    return lax.div(value, size), lax.rem(value, size)


def pack_kernel(dims, density, targets, cols, inner, *refs):
    local_rows, slots, side, strip_rows, meta_rows = dims
    per = slots // 3
    data = local_rows * per * side
    outs, (targets_v, cols_s, sems, meta_sems) = refs[:3], refs[3:]
    arrivals = [
        pltpu.make_async_copy(targets, targets_v, meta_sems.at[0]),
        pltpu.make_async_copy(cols, cols_s, meta_sems.at[1]),
    ]
    for arrival in arrivals:
        arrival.start()
    copies = []
    for group in (0, 2, 1):
        for row in range(local_rows):
            source = density.at[pl.ds((row * slots + group * per) * side, per * side)]
            dest = outs[group].at[pl.ds(row * per * side, per * side)]
            copies.append(pltpu.make_async_copy(source, dest, sems.at[group, row]))
            copies[-1].start()
    for group in (0, 2, 1):
        outs[group][data : data + meta_rows, :] = jnp.zeros((meta_rows, side), jnp.float32)
    for arrival in arrivals:
        arrival.wait()
    for group in (0, 2, 1):
        for row in range(local_rows):
            for slot in range(per):
                in_strip = parted(cols_s[row, group * per + slot], strip_rows)[1]
                owner, line = parted(in_strip, local_rows)
                code = (owner ^ inner[0]) * local_rows + line
                at = data + row * per + slot
                chosen = targets_v[group * per + slot, row : row + 1, :]
                outs[group][at : at + 1, :slots] = chosen.astype(jnp.float32)
                code = jnp.full((1, 1), code, jnp.int32).astype(jnp.float32)
                outs[group][at : at + 1, slots : slots + 1] = code
    for copy in copies:
        copy.wait()


def sums_kernel(dims, plan, *refs):
    offset, parts, local_rows, slots, side, meta_rows, a_at, group_total, first, width = dims
    per = slots // 3
    data = local_rows * per * side
    payloads = [refs[g * parts : (g + 1) * parts] for g in range(group_total)]
    *base, out, meta, listed, acc, meta_sems = refs[group_total * parts :]

    fetches = []
    for part in range(parts):
        source = payloads[a_at][part].at[pl.ds(data, meta_rows)]
        fetches.append(pltpu.make_async_copy(source, meta.at[part], meta_sems.at[part]))
        fetches[-1].start()
    acc[...] = jnp.zeros_like(acc)

    def cut(block):
        high = block.astype(jnp.bfloat16)
        return high, (block - high.astype(jnp.float32)).astype(jnp.bfloat16)

    for part in range(parts):
        fetches[part].wait()
        count = jnp.int32(0)
        for line in range(local_rows * per):
            dest = meta[part, line, slots].astype(jnp.int32) - (offset + part) * local_rows
            listed[0, count] = line
            listed[1, count] = line // per
            listed[2, count] = dest
            mine = (dest >= 0) & (dest < local_rows)
            count = count + mine.astype(jnp.int32)

        def multiply(item, _, part=part):
            line, row, dest = listed[0, item], listed[1, item], listed[2, item]
            start = pl.multiple_of(line * side, side)
            a_high, a_low = cut(payloads[a_at][part][pl.ds(start, side), :])
            a = jnp.concatenate([a_high, a_high, a_low], axis=0)
            for group, lane in plan:
                blocks = []
                for t in range(per):
                    start = pl.multiple_of((row * per + t) * side, side)
                    blocks.append(payloads[group][part][pl.ds(start, side), :])
                b_high, b_low = cut(jnp.concatenate(blocks, axis=1))
                b = jnp.concatenate([b_high, b_low, b_high], axis=0)
                result = lax.dot_general(a, b, TN, preferred_element_type=jnp.float32)
                for t in range(per):
                    target = meta[part, line, lane + t].astype(jnp.int32)
                    place = jnp.minimum(target - first, width)
                    acc[dest, place] += result[:, t * side : (t + 1) * side]
            return 0

        lax.fori_loop(0, count, multiply, 0)
    for row in range(local_rows):
        for t in range(width):
            if base and width == slots:
                out[row, t] = base[0][row, t] - acc[row, t]
            elif width == slots:
                start = (row * per + t % per) * side
                mine = payloads[t // per][0][start : start + side, :]
                out[row, t] = 2.0 * mine - acc[row, t]
            else:
                start = (row * width + t) * side
                lines = slice(start, start + side)
                out[lines, :] = base[0][lines, :] + acc[row, t] if base else acc[row, t]


def finish_kernel(base, lower, middle, own_middle, upper, out, result, sems):
    local_rows, slots, side, _ = base.shape
    per = slots // 3
    copies = []
    for row in range(local_rows):
        for slot in range(per):
            start = (row * per + slot) * side
            lines = slice(start, start + side)
            result[row, slot] = base[row, slot] - lower[lines, :]
            both = middle[lines, :] + own_middle[lines, :]
            result[row, per + slot] = base[row, per + slot] - both
            result[row, 2 * per + slot] = base[row, 2 * per + slot] - upper[lines, :]
        copies.append(pltpu.make_async_copy(result.at[row], out.at[row], sems.at[row]))
        copies[-1].start()
    for copy in copies:
        copy.wait()


def shards(density, block_cols, targets):
    local_rows, slots, side, _ = density.shape
    per = slots // 3
    parts = lax.axis_size("inner")
    strip_rows = local_rows * parts
    meta_rows = local_rows * per + -(local_rows * per) % 8
    used_rows = local_rows * per * side + meta_rows
    payload_rows = used_rows + 3
    in_hbm = pl.BlockSpec(memory_space=pltpu.HBM)
    scalars = pl.BlockSpec(memory_space=pltpu.SMEM)
    vectors = pl.BlockSpec(memory_space=pltpu.VMEM)

    lower, middle, upper = pl.pallas_call(
        functools.partial(pack_kernel, (local_rows, slots, side, strip_rows, meta_rows)),
        out_shape=[jax.ShapeDtypeStruct((payload_rows, side), jnp.float32)] * 3,
        in_specs=[in_hbm, in_hbm, in_hbm, scalars],
        out_specs=[vectors] * 3,
        scratch_shapes=[
            pltpu.VMEM((slots, local_rows, slots), jnp.int32),
            pltpu.SMEM((local_rows, slots), jnp.int32),
            pltpu.SemaphoreType.DMA((3, local_rows)),
            pltpu.SemaphoreType.DMA((2,)),
        ],
        compiler_params=pltpu.CompilerParams(vmem_limit_bytes=52 << 20),
        name="pack",
    )(
        density.reshape(-1, side),
        jnp.transpose(targets, (1, 0, 2)),
        block_cols,
        lax.axis_index("inner").reshape(1),
    )

    spare = 10

    def sums(groups, a_at, plan, first, width, offset=0, base=()):
        held = len(groups[0])
        dims = (offset, held, local_rows, slots, side, meta_rows, a_at, len(groups), first, width)
        return pl.pallas_call(
            functools.partial(sums_kernel, dims, plan),
            out_shape=jax.ShapeDtypeStruct(
                (local_rows * per * side + spare, side) if width == per else density.shape,
                jnp.float32,
            ),
            in_specs=[vectors] * (held * len(groups) + len(base)),
            out_specs=vectors,
            scratch_shapes=[
                pltpu.SMEM((held, meta_rows, side), jnp.float32),
                pltpu.SMEM((3, local_rows * per + 1), jnp.int32),
                pltpu.VMEM((local_rows, width + 1, side, side), jnp.float32),
                pltpu.SemaphoreType.DMA((held,)),
            ],
            compiler_params=pltpu.CompilerParams(vmem_limit_bytes=16 << 20),
            cost_estimate=pl.CostEstimate(flops=1, bytes_accessed=1, transcendentals=0),
            name="sums",
        )(*[payload for group in groups for payload in group], *base)

    def strip_sums(groups, a_at, plan, first):
        early = parts // 2 + 1
        total = sums([group[:early] for group in groups], a_at, plan, first, per)
        if parts > early:
            rest = [group[early:] for group in groups]
            total = sums(rest, a_at, plan, first, per, early, [total])
        return total

    def spread(far):
        return [one for value in far for one in halves(value[:used_rows])]

    def tied(values, *after):
        return list(lax.optimization_barrier((*values, *after)))[: len(values)]

    own_plan = ((0, 0), (1, per), (2, 2 * per))
    above = shifted(lower, -1)
    lowers, middles, uppers = halves(lower), halves(middle), halves(upper)
    far_upper = across(upper)
    base = sums([lowers, middles, uppers], 1, own_plan, 0, slots)

    far_middle = across(middle, [base])
    far_uppers = spread(far_upper)
    far_uppers = far_uppers[:1] + [tied([one], above)[0] for one in far_uppers[1:]]
    below_own = strip_sums([uppers + far_uppers], 0, ((0, 2 * per),), per)

    far_lower = across(lower, [below_own])
    to_below_own = shifted(below_own, 1)
    far_middles = spread(tied(far_middle, below_own))
    all_middles = middles + far_middles
    below_next = strip_sums([uppers + far_uppers, all_middles], 0, ((1, per),), 0)

    aboves = halves(above)
    far_above = across(above, [below_next, *aboves])
    to_below_next = shifted(below_next, 1)
    far_lowers = spread(tied(far_lower, below_next, to_below_own))
    above_next = strip_sums([lowers + far_lowers, all_middles], 0, ((1, per),), 2 * per)
    to_above_next = shifted(above_next, -1)
    if far_lowers:
        near = len(lowers)
        groups = [far_lowers, far_middles, far_uppers]
        base = sums(groups, 1, own_plan, 0, slots, near, [base])
        far_above = tied(far_above, base, above_next, to_below_next)
    aboves = aboves + spread(far_above)
    from_above = strip_sums([aboves], 0, ((0, 0),), per)
    return pl.pallas_call(
        finish_kernel,
        out_shape=jax.ShapeDtypeStruct(density.shape, jnp.float32),
        in_specs=[vectors] * 5,
        out_specs=in_hbm,
        scratch_shapes=[
            pltpu.VMEM(density.shape, jnp.float32),
            pltpu.SemaphoreType.DMA((local_rows,)),
        ],
        compiler_params=pltpu.CompilerParams(vmem_limit_bytes=16 << 20),
        cost_estimate=pl.CostEstimate(flops=1, bytes_accessed=1, transcendentals=0),
        name="finish",
    )(base, to_below_next, to_below_own, from_above, to_above_next)


def solution(mesh):
    return jax.shard_map(
        shards,
        mesh=mesh,
        in_specs=(
            P(("blk", "inner"), None, None, None),
            P(("blk", "inner"), None),
            P(("blk", "inner"), None, None),
        ),
        out_specs=P(("blk", "inner"), None, None, None),
        check_vma=False,
    )
```

```python
import functools

import jax
import jax.numpy as jnp
from jax import lax
from jax.experimental import pallas as pl
from jax.experimental.pallas import tpu as pltpu
from jax.sharding import PartitionSpec as P

TN = (((0,), (0,)), ((), ()))


def shifted(value, steps):
    count = lax.axis_size("blk")
    pairs = [(source, (source + steps) % count) for source in range(count)]
    return lax.ppermute(value, "blk", pairs)


def shifted_aslant(value, steps):
    count, width = lax.axis_size("blk"), lax.axis_size("inner")
    if width == 1:
        return shifted(value, steps)
    pairs = [
        (s * width + i, (s + steps) % count * width + (i ^ 1))
        for s in range(count)
        for i in range(width)
    ]
    return lax.ppermute(value, ("blk", "inner"), pairs)


def swapped(value, distance):
    count = lax.axis_size("inner")
    return lax.ppermute(value, "inner", [(i, i ^ distance) for i in range(count)])


def halves(value):
    held = [value]
    for bit in [1 << i for i in range(20) if (1 << i) < lax.axis_size("inner") // 2]:
        held = held + [swapped(one, bit) for one in held]
    return held


def across(value, after=()):
    count = lax.axis_size("inner")
    value = lax.optimization_barrier((value, *after))[0] if after else value
    return [swapped(value, count // 2)] if count > 1 else []


def parted(value, size):
    if size & (size - 1) == 0:
        return value >> (size.bit_length() - 1), value & (size - 1)
    return lax.div(value, size), lax.rem(value, size)


def pack_kernel(dims, density, targets, cols, inner, *refs):
    local_rows, slots, side, strip_rows, meta_rows = dims
    per = slots // 3
    data = local_rows * per * side
    outs, (targets_v, cols_s, sems, meta_sems) = refs[:3], refs[3:]
    arrivals = [
        pltpu.make_async_copy(targets, targets_v, meta_sems.at[0]),
        pltpu.make_async_copy(cols, cols_s, meta_sems.at[1]),
    ]
    for arrival in arrivals:
        arrival.start()
    copies = []
    for group in (0, 2, 1):
        for row in range(local_rows):
            source = density.at[pl.ds((row * slots + group * per) * side, per * side)]
            dest = outs[group].at[pl.ds(row * per * side, per * side)]
            copies.append(pltpu.make_async_copy(source, dest, sems.at[group, row]))
            copies[-1].start()
    for group in (0, 2, 1):
        outs[group][data : data + meta_rows, :] = jnp.zeros((meta_rows, side), jnp.float32)
    for arrival in arrivals:
        arrival.wait()
    for group in (0, 2, 1):
        for row in range(local_rows):
            for slot in range(per):
                in_strip = parted(cols_s[row, group * per + slot], strip_rows)[1]
                owner, line = parted(in_strip, local_rows)
                code = (owner ^ inner[0]) * local_rows + line
                at = data + row * per + slot
                chosen = targets_v[group * per + slot, row : row + 1, :]
                outs[group][at : at + 1, :slots] = chosen.astype(jnp.float32)
                code = jnp.full((1, 1), code, jnp.int32).astype(jnp.float32)
                outs[group][at : at + 1, slots : slots + 1] = code
    for copy in copies:
        copy.wait()


def cut(block):
    high = block.astype(jnp.bfloat16)
    return high, (block - high.astype(jnp.float32)).astype(jnp.bfloat16)


def multiplied(a, blocks):
    a_high, a_low = cut(a)
    b_high, b_low = cut(jnp.concatenate(blocks, axis=1))
    a = jnp.concatenate([a_high, a_high, a_low], axis=0)
    b = jnp.concatenate([b_high, b_low, b_high], axis=0)
    return lax.dot_general(a, b, TN, preferred_element_type=jnp.float32)


def partial_kernel(dims, below, above, *refs):
    parts, local_rows, slots, side, meta_rows = dims
    per = slots // 3
    data = local_rows * per * side
    outs, (meta, acc, meta_sems) = refs[:parts], refs[parts:]
    fetches = []
    for index, payload in enumerate((below, above)):
        source = payload.at[pl.ds(data, meta_rows)]
        fetches.append(pltpu.make_async_copy(source, meta.at[index], meta_sems.at[index]))
        fetches[-1].start()
    acc[...] = jnp.zeros_like(acc)
    for index, (payload, lane) in enumerate(((below, 2 * per), (above, 0))):
        fetches[index].wait()
        for line in range(local_rows * per):
            first = line // per * per
            blocks = [payload[t * side : (t + 1) * side, :] for t in range(first, first + per)]
            result = multiplied(payload[line * side : (line + 1) * side, :], blocks)
            dest = meta[index, line, slots].astype(jnp.int32)
            for t in range(per):
                target = meta[index, line, lane + t].astype(jnp.int32)
                place = jnp.minimum(target - per, per)
                acc[dest, place] += result[:, t * side : (t + 1) * side]
    for part in range(parts):
        for row in range(local_rows):
            for t in range(per):
                start = (row * per + t) * side
                outs[part][start : start + side, :] = acc[part * local_rows + row, t]


def sums_kernel(dims, plan, *refs):
    offset, parts, local_rows, slots, side, meta_rows, a_at, group_total, first, width = dims
    per = slots // 3
    data = local_rows * per * side
    payloads = [refs[g * parts : (g + 1) * parts] for g in range(group_total)]
    *base, out, meta, listed, acc, meta_sems = refs[group_total * parts :]

    fetches = []
    for part in range(parts):
        source = payloads[a_at][part].at[pl.ds(data, meta_rows)]
        fetches.append(pltpu.make_async_copy(source, meta.at[part], meta_sems.at[part]))
        fetches[-1].start()
    acc[...] = jnp.zeros_like(acc)

    for part in range(parts):
        fetches[part].wait()
        count = jnp.int32(0)
        for line in range(local_rows * per):
            dest = meta[part, line, slots].astype(jnp.int32) - (offset + part) * local_rows
            listed[0, count] = line
            listed[1, count] = line // per
            listed[2, count] = dest
            mine = (dest >= 0) & (dest < local_rows)
            count = count + mine.astype(jnp.int32)

        def multiply(item, _, part=part):
            line, row, dest = listed[0, item], listed[1, item], listed[2, item]
            start = pl.multiple_of(line * side, side)
            a = payloads[a_at][part][pl.ds(start, side), :]
            for group, lane in plan:
                blocks = []
                for t in range(per):
                    start = pl.multiple_of((row * per + t) * side, side)
                    blocks.append(payloads[group][part][pl.ds(start, side), :])
                result = multiplied(a, blocks)
                for t in range(per):
                    target = meta[part, line, lane + t].astype(jnp.int32)
                    place = jnp.minimum(target - first, width)
                    acc[dest, place] += result[:, t * side : (t + 1) * side]
            return 0

        lax.fori_loop(0, count, multiply, 0)
    for row in range(local_rows):
        for t in range(width):
            if base and width == slots:
                out[row, t] = base[0][row, t] - acc[row, t]
            elif width == slots:
                start = (row * per + t % per) * side
                mine = payloads[t // per][0][start : start + side, :]
                out[row, t] = 2.0 * mine - acc[row, t]
            else:
                start = (row * width + t) * side
                lines = slice(start, start + side)
                out[lines, :] = base[0][lines, :] + acc[row, t] if base else acc[row, t]


def finish_kernel(base, lower, upper, *refs):
    middles, (out, result, sems) = refs[:-3], refs[-3:]
    local_rows, slots, side, _ = base.shape
    per = slots // 3
    copies = []
    for row in range(local_rows):
        for slot in range(per):
            start = (row * per + slot) * side
            lines = slice(start, start + side)
            result[row, slot] = base[row, slot] - lower[lines, :]
            total = sum(middle[lines, :] for middle in middles)
            result[row, per + slot] = base[row, per + slot] - total
            result[row, 2 * per + slot] = base[row, 2 * per + slot] - upper[lines, :]
        copies.append(pltpu.make_async_copy(result.at[row], out.at[row], sems.at[row]))
        copies[-1].start()
    for copy in copies:
        copy.wait()


def shards(density, block_cols, targets):
    local_rows, slots, side, _ = density.shape
    per = slots // 3
    parts = lax.axis_size("inner")
    strip_rows = local_rows * parts
    meta_rows = local_rows * per + -(local_rows * per) % 8
    used_rows = local_rows * per * side + meta_rows
    payload_rows = used_rows + 3
    in_hbm = pl.BlockSpec(memory_space=pltpu.HBM)
    scalars = pl.BlockSpec(memory_space=pltpu.SMEM)
    vectors = pl.BlockSpec(memory_space=pltpu.VMEM)

    lower, middle, upper = pl.pallas_call(
        functools.partial(pack_kernel, (local_rows, slots, side, strip_rows, meta_rows)),
        out_shape=[jax.ShapeDtypeStruct((payload_rows, side), jnp.float32)] * 3,
        in_specs=[in_hbm, in_hbm, in_hbm, scalars],
        out_specs=[vectors] * 3,
        scratch_shapes=[
            pltpu.VMEM((slots, local_rows, slots), jnp.int32),
            pltpu.SMEM((local_rows, slots), jnp.int32),
            pltpu.SemaphoreType.DMA((3, local_rows)),
            pltpu.SemaphoreType.DMA((2,)),
        ],
        compiler_params=pltpu.CompilerParams(vmem_limit_bytes=52 << 20),
        name="pack",
    )(
        density.reshape(-1, side),
        jnp.transpose(targets, (1, 0, 2)),
        block_cols,
        lax.axis_index("inner").reshape(1),
    )

    spare = 10

    def sums(groups, a_at, plan, first, width, offset=0, base=()):
        held = len(groups[0])
        dims = (offset, held, local_rows, slots, side, meta_rows, a_at, len(groups), first, width)
        return pl.pallas_call(
            functools.partial(sums_kernel, dims, plan),
            out_shape=jax.ShapeDtypeStruct(
                (local_rows * per * side + spare, side) if width == per else density.shape,
                jnp.float32,
            ),
            in_specs=[vectors] * (held * len(groups) + len(base)),
            out_specs=vectors,
            scratch_shapes=[
                pltpu.SMEM((held, meta_rows, side), jnp.float32),
                pltpu.SMEM((3, local_rows * per + 1), jnp.int32),
                pltpu.VMEM((local_rows, width + 1, side, side), jnp.float32),
                pltpu.SemaphoreType.DMA((held,)),
            ],
            compiler_params=pltpu.CompilerParams(vmem_limit_bytes=16 << 20),
            cost_estimate=pl.CostEstimate(flops=1, bytes_accessed=1, transcendentals=0),
            name="sums",
        )(*[payload for group in groups for payload in group], *base)

    def strip_sums(groups, a_at, plan, first):
        early = parts // 2 + 1
        total = sums([group[:early] for group in groups], a_at, plan, first, per)
        if parts > early:
            rest = [group[early:] for group in groups]
            total = sums(rest, a_at, plan, first, per, early, [total])
        return total

    def spread(far):
        return [one for value in far for one in halves(value[:used_rows])]

    def tied(values, *after):
        return list(lax.optimization_barrier((*values, *after)))[: len(values)]

    def partials(below, above):
        return pl.pallas_call(
            functools.partial(partial_kernel, (parts, local_rows, slots, side, meta_rows)),
            out_shape=[
                jax.ShapeDtypeStruct((local_rows * per * side + spare, side), jnp.float32)
            ] * parts,
            in_specs=[vectors] * 2,
            out_specs=[vectors] * parts,
            scratch_shapes=[
                pltpu.SMEM((2, meta_rows, side), jnp.float32),
                pltpu.VMEM((strip_rows, per + 1, side, side), jnp.float32),
                pltpu.SemaphoreType.DMA((2,)),
            ],
            compiler_params=pltpu.CompilerParams(vmem_limit_bytes=16 << 20),
            cost_estimate=pl.CostEstimate(flops=1, bytes_accessed=1, transcendentals=0),
            name="partials",
        )(below, above)

    own_plan = ((0, 0), (1, per), (2, 2 * per))
    below, above = shifted(upper, 1), shifted(lower, -1)
    lowers, middles, uppers = halves(lower), halves(middle), halves(upper)
    far_middle = across(middle)
    base = sums([lowers, middles, uppers], 1, own_plan, 0, slots)

    far_upper = across(upper, [base])
    far_middles = spread(far_middle)
    far_lower = across(lower, [*far_middles, below, above])
    all_middles = middles + far_middles
    far_uppers = spread(far_upper)
    below_next = strip_sums([uppers + far_uppers, all_middles], 0, ((1, per),), 0)
    to_below_next = shifted_aslant(below_next, 1)

    shares = dict(enumerate(partials(below, above)))
    for bit in [1 << i for i in range(20) if (1 << i) < parts // 2]:
        shares = {
            distance: share + swapped(shares[distance ^ bit], bit)
            for distance, share in shares.items()
            if not distance & bit
        }
    far_share = across(shares[parts // 2], [below_next]) if parts > 1 else []
    far_lowers = spread(tied(far_lower, below_next)) if far_lower else []
    above_next = strip_sums([lowers + far_lowers, all_middles], 0, ((1, per),), 2 * per)
    to_above_next = shifted(above_next, -1)
    if far_lowers:
        near = len(lowers)
        groups = [far_lowers, far_middles, far_uppers]
        base = sums(groups, 1, own_plan, 0, slots, near, [base])
        to_below_next = swapped(to_below_next, 1)
    middle_shares = [shares[0], *far_share]
    return pl.pallas_call(
        finish_kernel,
        out_shape=jax.ShapeDtypeStruct(density.shape, jnp.float32),
        in_specs=[vectors] * (3 + len(middle_shares)),
        out_specs=in_hbm,
        scratch_shapes=[
            pltpu.VMEM(density.shape, jnp.float32),
            pltpu.SemaphoreType.DMA((local_rows,)),
        ],
        compiler_params=pltpu.CompilerParams(vmem_limit_bytes=16 << 20),
        cost_estimate=pl.CostEstimate(flops=1, bytes_accessed=1, transcendentals=0),
        name="finish",
    )(base, to_below_next, to_above_next, *middle_shares)


def solution(mesh):
    return jax.shard_map(
        shards,
        mesh=mesh,
        in_specs=(
            P(("blk", "inner"), None, None, None),
            P(("blk", "inner"), None),
            P(("blk", "inner"), None, None),
        ),
        out_specs=P(("blk", "inner"), None, None, None),
        check_vma=False,
    )
```

```python
import functools

import jax
import jax.numpy as jnp
from jax import lax
from jax.experimental import pallas as pl
from jax.experimental.pallas import tpu as pltpu
from jax.sharding import PartitionSpec as P

TN = (((0,), (0,)), ((), ()))


def shifted(value, steps):
    count = lax.axis_size("blk")
    pairs = [(source, (source + steps) % count) for source in range(count)]
    return lax.ppermute(value, "blk", pairs)


def shifted_aslant(value, steps):
    count, width = lax.axis_size("blk"), lax.axis_size("inner")
    if width == 1:
        return shifted(value, steps)
    pairs = [
        (s * width + i, (s + steps) % count * width + (i ^ 1))
        for s in range(count)
        for i in range(width)
    ]
    return lax.ppermute(value, ("blk", "inner"), pairs)


def swapped(value, distance):
    count = lax.axis_size("inner")
    return lax.ppermute(value, "inner", [(i, i ^ distance) for i in range(count)])


def halves(value):
    held = [value]
    for bit in [1 << i for i in range(20) if (1 << i) < lax.axis_size("inner") // 2]:
        held = held + [swapped(one, bit) for one in held]
    return held


def across(value, after=()):
    count = lax.axis_size("inner")
    value = lax.optimization_barrier((value, *after))[0] if after else value
    return [swapped(value, count // 2)] if count > 1 else []


def parted(value, size):
    if size & (size - 1) == 0:
        return value >> (size.bit_length() - 1), value & (size - 1)
    return lax.div(value, size), lax.rem(value, size)


def pack_kernel(dims, density, targets, cols, inner, *refs):
    local_rows, slots, side, strip_rows, meta_rows = dims
    per = slots // 3
    data = local_rows * per * side
    outs, (targets_v, cols_s, sems, meta_sems) = refs[:3], refs[3:]
    arrivals = [
        pltpu.make_async_copy(targets, targets_v, meta_sems.at[0]),
        pltpu.make_async_copy(cols, cols_s, meta_sems.at[1]),
    ]
    for arrival in arrivals:
        arrival.start()
    copies = []
    for group in (0, 2, 1):
        for row in range(local_rows):
            source = density.at[pl.ds((row * slots + group * per) * side, per * side)]
            dest = outs[group].at[pl.ds(row * per * side, per * side)]
            copies.append(pltpu.make_async_copy(source, dest, sems.at[group, row]))
            copies[-1].start()
    for group in (0, 2, 1):
        outs[group][data : data + meta_rows, :] = jnp.zeros((meta_rows, side), jnp.float32)
    for arrival in arrivals:
        arrival.wait()
    for group in (0, 2, 1):
        for row in range(local_rows):
            for slot in range(per):
                in_strip = parted(cols_s[row, group * per + slot], strip_rows)[1]
                owner, line = parted(in_strip, local_rows)
                code = (owner ^ inner[0]) * local_rows + line
                at = data + row * per + slot
                chosen = targets_v[group * per + slot, row : row + 1, :]
                outs[group][at : at + 1, :slots] = chosen.astype(jnp.float32)
                code = jnp.full((1, 1), code, jnp.int32).astype(jnp.float32)
                outs[group][at : at + 1, slots : slots + 1] = code
    for copy in copies:
        copy.wait()


def cut(block):
    high = block.astype(jnp.bfloat16)
    return high, (block - high.astype(jnp.float32)).astype(jnp.bfloat16)


def multiplied(a, blocks):
    a_high, a_low = cut(a)
    b_high, b_low = cut(jnp.concatenate(blocks, axis=1))
    a = jnp.concatenate([a_high, a_high, a_low], axis=0)
    b = jnp.concatenate([b_high, b_low, b_high], axis=0)
    return lax.dot_general(a, b, TN, preferred_element_type=jnp.float32)


def partial_kernel(dims, below, above, *refs):
    parts, local_rows, slots, side, meta_rows = dims
    per = slots // 3
    data = local_rows * per * side
    outs, (meta, acc, meta_sems) = refs[:parts], refs[parts:]
    fetches = []
    for index, payload in enumerate((below, above)):
        source = payload.at[pl.ds(data, meta_rows)]
        fetches.append(pltpu.make_async_copy(source, meta.at[index], meta_sems.at[index]))
        fetches[-1].start()
    acc[...] = jnp.zeros_like(acc)
    for index, (payload, lane) in enumerate(((below, 2 * per), (above, 0))):
        fetches[index].wait()
        for line in range(local_rows * per):
            first = line // per * per
            blocks = [payload[t * side : (t + 1) * side, :] for t in range(first, first + per)]
            result = multiplied(payload[line * side : (line + 1) * side, :], blocks)
            dest = meta[index, line, slots].astype(jnp.int32)
            for t in range(per):
                target = meta[index, line, lane + t].astype(jnp.int32)
                place = jnp.minimum(target - per, per)
                acc[dest, place] += result[:, t * side : (t + 1) * side]
    for part in range(parts):
        for row in range(local_rows):
            for t in range(per):
                start = (row * per + t) * side
                outs[part][start : start + side, :] = acc[part * local_rows + row, t]


def sums_kernel(dims, plan, *refs):
    offset, parts, local_rows, slots, side, meta_rows, a_at, group_total, first, width = dims
    per = slots // 3
    data = local_rows * per * side
    payloads = [refs[g * parts : (g + 1) * parts] for g in range(group_total)]
    *base, out, meta, listed, acc, meta_sems = refs[group_total * parts :]

    fetches = []
    for part in range(parts):
        source = payloads[a_at][part].at[pl.ds(data, meta_rows)]
        fetches.append(pltpu.make_async_copy(source, meta.at[part], meta_sems.at[part]))
        fetches[-1].start()
    acc[...] = jnp.zeros_like(acc)

    for part in range(parts):
        fetches[part].wait()
        count = jnp.int32(0)
        for line in range(local_rows * per):
            dest = meta[part, line, slots].astype(jnp.int32) - (offset + part) * local_rows
            listed[0, count] = line
            listed[1, count] = line // per
            listed[2, count] = dest
            mine = (dest >= 0) & (dest < local_rows)
            count = count + mine.astype(jnp.int32)

        def multiply(item, _, part=part):
            line, row, dest = listed[0, item], listed[1, item], listed[2, item]
            start = pl.multiple_of(line * side, side)
            a = payloads[a_at][part][pl.ds(start, side), :]
            for group, lane in plan:
                blocks = []
                for t in range(per):
                    start = pl.multiple_of((row * per + t) * side, side)
                    blocks.append(payloads[group][part][pl.ds(start, side), :])
                result = multiplied(a, blocks)
                for t in range(per):
                    target = meta[part, line, lane + t].astype(jnp.int32)
                    place = jnp.minimum(target - first, width)
                    acc[dest, place] += result[:, t * side : (t + 1) * side]
            return 0

        lax.fori_loop(0, count, multiply, 0)
    for row in range(local_rows):
        for t in range(width):
            if base and width == slots:
                out[row, t] = base[0][row, t] - acc[row, t]
            elif width == slots:
                start = (row * per + t % per) * side
                mine = payloads[t // per][0][start : start + side, :]
                out[row, t] = 2.0 * mine - acc[row, t]
            else:
                start = (row * width + t) * side
                lines = slice(start, start + side)
                out[lines, :] = base[0][lines, :] + acc[row, t] if base else acc[row, t]


def finish_kernel(base, lower, upper, *refs):
    middles, (out, result, sems) = refs[:-3], refs[-3:]
    local_rows, slots, side, _ = base.shape
    per = slots // 3
    copies = []
    for row in range(local_rows):
        for slot in range(per):
            start = (row * per + slot) * side
            lines = slice(start, start + side)
            result[row, slot] = base[row, slot] - lower[lines, :]
            total = sum(middle[lines, :] for middle in middles)
            result[row, per + slot] = base[row, per + slot] - total
            result[row, 2 * per + slot] = base[row, 2 * per + slot] - upper[lines, :]
        copies.append(pltpu.make_async_copy(result.at[row], out.at[row], sems.at[row]))
        copies[-1].start()
    for copy in copies:
        copy.wait()


def shards(density, block_cols, targets):
    local_rows, slots, side, _ = density.shape
    per = slots // 3
    parts = lax.axis_size("inner")
    strip_rows = local_rows * parts
    meta_rows = local_rows * per + -(local_rows * per) % 8
    used_rows = local_rows * per * side + meta_rows
    payload_rows = used_rows + 7
    in_hbm = pl.BlockSpec(memory_space=pltpu.HBM)
    scalars = pl.BlockSpec(memory_space=pltpu.SMEM)
    vectors = pl.BlockSpec(memory_space=pltpu.VMEM)

    lower, middle, upper = pl.pallas_call(
        functools.partial(pack_kernel, (local_rows, slots, side, strip_rows, meta_rows)),
        out_shape=[jax.ShapeDtypeStruct((payload_rows, side), jnp.float32)] * 3,
        in_specs=[in_hbm, in_hbm, in_hbm, scalars],
        out_specs=[vectors] * 3,
        scratch_shapes=[
            pltpu.VMEM((slots, local_rows, slots), jnp.int32),
            pltpu.SMEM((local_rows, slots), jnp.int32),
            pltpu.SemaphoreType.DMA((3, local_rows)),
            pltpu.SemaphoreType.DMA((2,)),
        ],
        compiler_params=pltpu.CompilerParams(vmem_limit_bytes=52 << 20),
        name="pack",
    )(
        density.reshape(-1, side),
        jnp.transpose(targets, (1, 0, 2)),
        block_cols,
        lax.axis_index("inner").reshape(1),
    )

    lines = local_rows * per * side

    def sums(groups, a_at, plan, first, width, offset=0, base=(), spare=0):
        held = len(groups[0])
        dims = (offset, held, local_rows, slots, side, meta_rows, a_at, len(groups), first, width)
        return pl.pallas_call(
            functools.partial(sums_kernel, dims, plan),
            out_shape=jax.ShapeDtypeStruct(
                (lines + spare, side) if width == per else density.shape,
                jnp.float32,
            ),
            in_specs=[vectors] * (held * len(groups) + len(base)),
            out_specs=vectors,
            scratch_shapes=[
                pltpu.SMEM((held, meta_rows, side), jnp.float32),
                pltpu.SMEM((3, local_rows * per + 1), jnp.int32),
                pltpu.VMEM((local_rows, width + 1, side, side), jnp.float32),
                pltpu.SemaphoreType.DMA((held,)),
            ],
            compiler_params=pltpu.CompilerParams(vmem_limit_bytes=16 << 20),
            cost_estimate=pl.CostEstimate(flops=1, bytes_accessed=1, transcendentals=0),
            name="sums",
        )(*[payload for group in groups for payload in group], *base)

    def strip_sums(groups, a_at, plan, first, spare):
        early = parts // 2 + 1
        total = sums([group[:early] for group in groups], a_at, plan, first, per, spare=spare)
        if parts > early:
            rest = [group[early:] for group in groups]
            total = sums(rest, a_at, plan, first, per, early, [total], spare)
        return total

    def spread(far):
        return [one for value in far for one in halves(value[:used_rows])]

    def tied(values, *after):
        return list(lax.optimization_barrier((*values, *after)))[: len(values)]

    def partials(below, above):
        return pl.pallas_call(
            functools.partial(partial_kernel, (parts, local_rows, slots, side, meta_rows)),
            out_shape=[
                jax.ShapeDtypeStruct((lines + 10, side), jnp.float32)
            ] * parts,
            in_specs=[vectors] * 2,
            out_specs=[vectors] * parts,
            scratch_shapes=[
                pltpu.SMEM((2, meta_rows, side), jnp.float32),
                pltpu.VMEM((strip_rows, per + 1, side, side), jnp.float32),
                pltpu.SemaphoreType.DMA((2,)),
            ],
            compiler_params=pltpu.CompilerParams(vmem_limit_bytes=16 << 20),
            cost_estimate=pl.CostEstimate(flops=1, bytes_accessed=1, transcendentals=0),
            name="partials",
        )(below, above)

    own_plan = ((0, 0), (1, per), (2, 2 * per))
    below, above = shifted(upper, 1), shifted(lower, -1)
    lowers, middles, uppers = halves(lower), halves(middle), halves(upper)
    far_middle = across(middle)
    base = sums([lowers, middles, uppers], 1, own_plan, 0, slots)

    far_upper = across(upper, [base])
    far_middles = spread(far_middle)
    far_lower = across(lower, far_middles)
    all_middles = middles + far_middles
    far_uppers = spread(tied(far_upper, below, above))
    below_next = strip_sums([uppers + far_uppers, all_middles], 0, ((1, per),), 0, 22)
    to_below_next = shifted_aslant(below_next, 1)

    shares = dict(enumerate(partials(*tied([below, above], below_next))))
    for bit in [1 << i for i in range(20) if (1 << i) < parts // 2]:
        shares = {
            distance: share + swapped(shares[distance ^ bit], bit)
            for distance, share in shares.items()
            if not distance & bit
        }
    far_share = across(shares[parts // 2], [below_next]) if parts > 1 else []
    far_lowers = spread(tied(far_lower, below_next)) if far_lower else []
    above_next = strip_sums([lowers + far_lowers, all_middles], 0, ((1, per),), 2 * per, 9)
    to_above_next = shifted(above_next, -1)
    if far_lowers:
        near = len(lowers)
        groups = [far_lowers, far_middles, far_uppers]
        base = sums(groups, 1, own_plan, 0, slots, near, [base])
        to_below_next = swapped(to_below_next[:lines], 1)
    middle_shares = [shares[0], *far_share]
    return pl.pallas_call(
        finish_kernel,
        out_shape=jax.ShapeDtypeStruct(density.shape, jnp.float32),
        in_specs=[vectors] * (3 + len(middle_shares)),
        out_specs=in_hbm,
        scratch_shapes=[
            pltpu.VMEM(density.shape, jnp.float32),
            pltpu.SemaphoreType.DMA((local_rows,)),
        ],
        compiler_params=pltpu.CompilerParams(vmem_limit_bytes=16 << 20),
        cost_estimate=pl.CostEstimate(flops=1, bytes_accessed=1, transcendentals=0),
        name="finish",
    )(base, to_below_next, to_above_next, *middle_shares)


def solution(mesh):
    return jax.shard_map(
        shards,
        mesh=mesh,
        in_specs=(
            P(("blk", "inner"), None, None, None),
            P(("blk", "inner"), None),
            P(("blk", "inner"), None, None),
        ),
        out_specs=P(("blk", "inner"), None, None, None),
        check_vma=False,
    )
```

```python
import functools

import jax
import jax.numpy as jnp
from jax import lax
from jax.experimental import pallas as pl
from jax.experimental.pallas import tpu as pltpu
from jax.sharding import PartitionSpec as P

TN = (((0,), (0,)), ((), ()))


def shifted(value, steps):
    count = lax.axis_size("blk")
    pairs = [(source, (source + steps) % count) for source in range(count)]
    return lax.ppermute(value, "blk", pairs)


def shifted_aslant(value, steps):
    count, width = lax.axis_size("blk"), lax.axis_size("inner")
    if width == 1:
        return shifted(value, steps)
    pairs = [
        (s * width + i, (s + steps) % count * width + (i ^ 1))
        for s in range(count)
        for i in range(width)
    ]
    return lax.ppermute(value, ("blk", "inner"), pairs)


def swapped(value, distance):
    count = lax.axis_size("inner")
    return lax.ppermute(value, "inner", [(i, i ^ distance) for i in range(count)])


def halves(value):
    held = [value]
    for bit in [1 << i for i in range(20) if (1 << i) < lax.axis_size("inner") // 2]:
        held = held + [swapped(one, bit) for one in held]
    return held


def across(value, after=()):
    count = lax.axis_size("inner")
    value = lax.optimization_barrier((value, *after))[0] if after else value
    return [swapped(value, count // 2)] if count > 1 else []


def parted(value, size):
    if size & (size - 1) == 0:
        return value >> (size.bit_length() - 1), value & (size - 1)
    return lax.div(value, size), lax.rem(value, size)


def pack_kernel(dims, density, codes, inner, *refs):
    local_rows, slots, side, strip_rows, meta_rows = dims
    per = slots // 3
    data = local_rows * per * side
    outs, sems = refs[:3], refs[3]
    copies = []
    for group in (0, 2, 1):
        for row in range(local_rows):
            source = density.at[pl.ds((row * slots + group * per) * side, per * side)]
            dest = outs[group].at[pl.ds(row * per * side, per * side)]
            copies.append(pltpu.make_async_copy(source, dest, sems.at[group, row]))
            copies[-1].start()
    for group in (0, 2, 1):
        outs[group][data : data + meta_rows, :] = jnp.zeros((meta_rows, side), jnp.float32)
    lanes = lax.broadcasted_iota(jnp.int32, (local_rows, slots), 1)
    owner, place = parted(parted(codes[slots], strip_rows)[1], local_rows)
    dests = ((owner ^ inner[0]) * local_rows + place).astype(jnp.float32)
    for group in (0, 2, 1):
        for slot in range(per):
            chosen = codes[group * per + slot].astype(jnp.float32)
            mine = jnp.where(lanes == group * per + slot, dests, 0.0)
            dest = jnp.sum(mine, axis=1, keepdims=True)
            for row in range(local_rows):
                at = data + row * per + slot
                outs[group][at : at + 1, :slots] = chosen[row : row + 1]
                outs[group][at : at + 1, slots : slots + 1] = dest[row : row + 1]
    for copy in copies:
        copy.wait()


def cut(block):
    high = block.astype(jnp.bfloat16)
    return high, (block - high.astype(jnp.float32)).astype(jnp.bfloat16)


def multiplied(a, blocks):
    a_high, a_low = cut(a)
    b_high, b_low = cut(jnp.concatenate(blocks, axis=1))
    a = jnp.concatenate([a_high, a_high, a_low], axis=0)
    b = jnp.concatenate([b_high, b_low, b_high], axis=0)
    return lax.dot_general(a, b, TN, preferred_element_type=jnp.float32)


def partial_kernel(dims, below, above, *refs):
    parts, local_rows, slots, side, meta_rows = dims
    per = slots // 3
    data = local_rows * per * side
    outs, (meta, acc, meta_sems) = refs[:parts], refs[parts:]
    fetches = []
    for index, payload in enumerate((below, above)):
        source = payload.at[pl.ds(data, meta_rows)]
        fetches.append(pltpu.make_async_copy(source, meta.at[index], meta_sems.at[index]))
        fetches[-1].start()
    acc[...] = jnp.zeros_like(acc)
    for index, (payload, lane) in enumerate(((below, 2 * per), (above, 0))):
        fetches[index].wait()
        for line in range(local_rows * per):
            first = line // per * per
            blocks = [payload[t * side : (t + 1) * side, :] for t in range(first, first + per)]
            result = multiplied(payload[line * side : (line + 1) * side, :], blocks)
            dest = meta[index, line, slots].astype(jnp.int32)
            for t in range(per):
                target = meta[index, line, lane + t].astype(jnp.int32)
                place = jnp.minimum(target - per, per)
                acc[dest, place] += result[:, t * side : (t + 1) * side]
    for part in range(parts):
        for row in range(local_rows):
            for t in range(per):
                start = (row * per + t) * side
                outs[part][start : start + side, :] = acc[part * local_rows + row, t]


def sums_kernel(dims, plan, *refs):
    offset, parts, local_rows, slots, side, meta_rows, a_at, group_total, first, width = dims
    per = slots // 3
    data = local_rows * per * side
    payloads = [refs[g * parts : (g + 1) * parts] for g in range(group_total)]
    *base, out, meta, listed, acc, meta_sems = refs[group_total * parts :]

    fetches = []
    for part in range(parts):
        source = payloads[a_at][part].at[pl.ds(data, meta_rows)]
        fetches.append(pltpu.make_async_copy(source, meta.at[part], meta_sems.at[part]))
        fetches[-1].start()
    acc[...] = jnp.zeros_like(acc)

    for part in range(parts):
        fetches[part].wait()
        count = jnp.int32(0)
        for line in range(local_rows * per):
            dest = meta[part, line, slots].astype(jnp.int32) - (offset + part) * local_rows
            listed[0, count] = line
            listed[1, count] = line // per
            listed[2, count] = dest
            mine = (dest >= 0) & (dest < local_rows)
            count = count + mine.astype(jnp.int32)

        def multiply(item, _, part=part):
            line, row, dest = listed[0, item], listed[1, item], listed[2, item]
            start = pl.multiple_of(line * side, side)
            a = payloads[a_at][part][pl.ds(start, side), :]
            for group, lane in plan:
                blocks = []
                for t in range(per):
                    start = pl.multiple_of((row * per + t) * side, side)
                    blocks.append(payloads[group][part][pl.ds(start, side), :])
                result = multiplied(a, blocks)
                for t in range(per):
                    target = meta[part, line, lane + t].astype(jnp.int32)
                    place = jnp.minimum(target - first, width)
                    acc[dest, place] += result[:, t * side : (t + 1) * side]
            return 0

        lax.fori_loop(0, count, multiply, 0)
    for row in range(local_rows):
        for t in range(width):
            if base and width == slots:
                out[row, t] = base[0][row, t] - acc[row, t]
            elif width == slots:
                start = (row * per + t % per) * side
                mine = payloads[t // per][0][start : start + side, :]
                out[row, t] = 2.0 * mine - acc[row, t]
            else:
                start = (row * width + t) * side
                lines = slice(start, start + side)
                out[lines, :] = base[0][lines, :] + acc[row, t] if base else acc[row, t]


def finish_kernel(base, lower, upper, *refs):
    middles, (out, result, sems) = refs[:-3], refs[-3:]
    local_rows, slots, side, _ = base.shape
    per = slots // 3
    copies = []
    for row in range(local_rows):
        for slot in range(per):
            start = (row * per + slot) * side
            lines = slice(start, start + side)
            result[row, slot] = base[row, slot] - lower[lines, :]
            total = sum(middle[lines, :] for middle in middles)
            result[row, per + slot] = base[row, per + slot] - total
            result[row, 2 * per + slot] = base[row, 2 * per + slot] - upper[lines, :]
        copies.append(pltpu.make_async_copy(result.at[row], out.at[row], sems.at[row]))
        copies[-1].start()
    for copy in copies:
        copy.wait()


def shards(density, block_cols, targets):
    local_rows, slots, side, _ = density.shape
    per = slots // 3
    parts = lax.axis_size("inner")
    strip_rows = local_rows * parts
    meta_rows = local_rows * per + -(local_rows * per) % 8
    used_rows = local_rows * per * side + meta_rows
    payload_rows = used_rows + 7
    in_hbm = pl.BlockSpec(memory_space=pltpu.HBM)
    scalars = pl.BlockSpec(memory_space=pltpu.SMEM)
    vectors = pl.BlockSpec(memory_space=pltpu.VMEM)

    codes = jnp.concatenate([jnp.transpose(targets, (1, 0, 2)), block_cols[None]], axis=0)
    lower, middle, upper = pl.pallas_call(
        functools.partial(pack_kernel, (local_rows, slots, side, strip_rows, meta_rows)),
        out_shape=[jax.ShapeDtypeStruct((payload_rows, side), jnp.float32)] * 3,
        in_specs=[in_hbm, vectors, scalars],
        out_specs=[vectors] * 3,
        scratch_shapes=[
            pltpu.SemaphoreType.DMA((3, local_rows)),
        ],
        compiler_params=pltpu.CompilerParams(vmem_limit_bytes=52 << 20),
        name="pack",
    )(
        density.reshape(-1, side),
        codes,
        lax.axis_index("inner").reshape(1),
    )

    lines = local_rows * per * side

    def sums(groups, a_at, plan, first, width, offset=0, base=(), spare=0):
        held = len(groups[0])
        dims = (offset, held, local_rows, slots, side, meta_rows, a_at, len(groups), first, width)
        return pl.pallas_call(
            functools.partial(sums_kernel, dims, plan),
            out_shape=jax.ShapeDtypeStruct(
                (lines + spare, side) if width == per else density.shape,
                jnp.float32,
            ),
            in_specs=[vectors] * (held * len(groups) + len(base)),
            out_specs=vectors,
            scratch_shapes=[
                pltpu.SMEM((held, meta_rows, side), jnp.float32),
                pltpu.SMEM((3, local_rows * per + 1), jnp.int32),
                pltpu.VMEM((local_rows, width + 1, side, side), jnp.float32),
                pltpu.SemaphoreType.DMA((held,)),
            ],
            compiler_params=pltpu.CompilerParams(vmem_limit_bytes=16 << 20),
            cost_estimate=pl.CostEstimate(flops=1, bytes_accessed=1, transcendentals=0),
            name="sums",
        )(*[payload for group in groups for payload in group], *base)

    def strip_sums(groups, a_at, plan, first, spare):
        early = parts // 2 + 1
        total = sums([group[:early] for group in groups], a_at, plan, first, per, spare=spare)
        if parts > early:
            rest = [group[early:] for group in groups]
            total = sums(rest, a_at, plan, first, per, early, [total], spare)
        return total

    def spread(far):
        return [one for value in far for one in halves(value[:used_rows])]

    def tied(values, *after):
        return list(lax.optimization_barrier((*values, *after)))[: len(values)]

    def partials(below, above):
        return pl.pallas_call(
            functools.partial(partial_kernel, (parts, local_rows, slots, side, meta_rows)),
            out_shape=[
                jax.ShapeDtypeStruct((lines + 10, side), jnp.float32)
            ] * parts,
            in_specs=[vectors] * 2,
            out_specs=[vectors] * parts,
            scratch_shapes=[
                pltpu.SMEM((2, meta_rows, side), jnp.float32),
                pltpu.VMEM((strip_rows, per + 1, side, side), jnp.float32),
                pltpu.SemaphoreType.DMA((2,)),
            ],
            compiler_params=pltpu.CompilerParams(vmem_limit_bytes=16 << 20),
            cost_estimate=pl.CostEstimate(flops=1, bytes_accessed=1, transcendentals=0),
            name="partials",
        )(below, above)

    own_plan = ((0, 0), (1, per), (2, 2 * per))
    below, above = shifted(upper, 1), shifted(lower, -1)
    lowers, middles, uppers = halves(lower), halves(middle), halves(upper)
    far_middle = across(middle)
    base = sums([lowers, middles, uppers], 1, own_plan, 0, slots)

    far_upper = across(upper, [base])
    far_middles = spread(far_middle)
    far_lower = across(lower, far_middles)
    all_middles = middles + far_middles
    far_uppers = spread(tied(far_upper, below, above))
    below_next = strip_sums([uppers + far_uppers, all_middles], 0, ((1, per),), 0, 22)
    to_below_next = shifted_aslant(below_next, 1)

    shares = dict(enumerate(partials(*tied([below, above], below_next))))
    for bit in [1 << i for i in range(20) if (1 << i) < parts // 2]:
        shares = {
            distance: share + swapped(shares[distance ^ bit], bit)
            for distance, share in shares.items()
            if not distance & bit
        }
    far_share = across(shares[parts // 2], [below_next]) if parts > 1 else []
    far_lowers = spread(tied(far_lower, below_next)) if far_lower else []
    above_next = strip_sums([lowers + far_lowers, all_middles], 0, ((1, per),), 2 * per, 9)
    to_above_next = shifted(above_next, -1)
    if far_lowers:
        near = len(lowers)
        groups = [far_lowers, far_middles, far_uppers]
        base = sums(groups, 1, own_plan, 0, slots, near, [base])
        to_below_next = swapped(to_below_next[:lines], 1)
    middle_shares = [shares[0], *far_share]
    return pl.pallas_call(
        finish_kernel,
        out_shape=jax.ShapeDtypeStruct(density.shape, jnp.float32),
        in_specs=[vectors] * (3 + len(middle_shares)),
        out_specs=in_hbm,
        scratch_shapes=[
            pltpu.VMEM(density.shape, jnp.float32),
            pltpu.SemaphoreType.DMA((local_rows,)),
        ],
        compiler_params=pltpu.CompilerParams(vmem_limit_bytes=16 << 20),
        cost_estimate=pl.CostEstimate(flops=1, bytes_accessed=1, transcendentals=0),
        name="finish",
    )(base, to_below_next, to_above_next, *middle_shares)


def solution(mesh):
    return jax.shard_map(
        shards,
        mesh=mesh,
        in_specs=(
            P(("blk", "inner"), None, None, None),
            P(("blk", "inner"), None),
            P(("blk", "inner"), None, None),
        ),
        out_specs=P(("blk", "inner"), None, None, None),
        check_vma=False,
    )
```

```python
import functools

import jax
import jax.numpy as jnp
from jax import lax
from jax.experimental import pallas as pl
from jax.experimental.pallas import tpu as pltpu
from jax.sharding import PartitionSpec as P

TN = (((0,), (0,)), ((), ()))


def shifted(value, steps):
    count = lax.axis_size("blk")
    pairs = [(source, (source + steps) % count) for source in range(count)]
    return lax.ppermute(value, "blk", pairs)


def shifted_aslant(value, steps):
    count, width = lax.axis_size("blk"), lax.axis_size("inner")
    if width == 1:
        return shifted(value, steps)
    pairs = [
        (s * width + i, (s + steps) % count * width + (i ^ 1))
        for s in range(count)
        for i in range(width)
    ]
    return lax.ppermute(value, ("blk", "inner"), pairs)


def swapped(value, distance):
    count = lax.axis_size("inner")
    return lax.ppermute(value, "inner", [(i, i ^ distance) for i in range(count)])


def halves(value):
    held = [value]
    for bit in [1 << i for i in range(20) if (1 << i) < lax.axis_size("inner") // 2]:
        held = held + [swapped(one, bit) for one in held]
    return held


def across(value, after=()):
    count = lax.axis_size("inner")
    value = lax.optimization_barrier((value, *after))[0] if after else value
    return [swapped(value, count // 2)] if count > 1 else []


def parted(value, size):
    if size & (size - 1) == 0:
        return value >> (size.bit_length() - 1), value & (size - 1)
    return lax.div(value, size), lax.rem(value, size)


def pack_kernel(dims, density, codes, inner, *refs):
    local_rows, slots, side, strip_rows, meta_rows = dims
    per = slots // 3
    data = local_rows * per * side
    outs, sems = refs[:3], refs[3]
    copies = []
    for group in (0, 2, 1):
        for row in range(local_rows):
            source = density.at[pl.ds((row * slots + group * per) * side, per * side)]
            dest = outs[group].at[pl.ds(row * per * side, per * side)]
            copies.append(pltpu.make_async_copy(source, dest, sems.at[group, row]))
            copies[-1].start()
    for group in (0, 2, 1):
        outs[group][data : data + meta_rows, :] = jnp.zeros((meta_rows, side), jnp.float32)
    lanes = lax.broadcasted_iota(jnp.int32, (local_rows, slots), 1)
    owner, place = parted(parted(codes[slots], strip_rows)[1], local_rows)
    dests = ((owner ^ inner[0]) * local_rows + place).astype(jnp.float32)
    for group in (0, 2, 1):
        for slot in range(per):
            chosen = codes[group * per + slot].astype(jnp.float32)
            mine = jnp.where(lanes == group * per + slot, dests, 0.0)
            dest = jnp.sum(mine, axis=1, keepdims=True)
            for row in range(local_rows):
                at = data + row * per + slot
                outs[group][at : at + 1, :slots] = chosen[row : row + 1]
                outs[group][at : at + 1, slots : slots + 1] = dest[row : row + 1]
    for copy in copies:
        copy.wait()


def cut(block):
    high = block.astype(jnp.bfloat16)
    return high, (block - high.astype(jnp.float32)).astype(jnp.bfloat16)


def multiplied(a, blocks):
    a_high, a_low = cut(a)
    b_high, b_low = cut(jnp.concatenate(blocks, axis=1))
    a = jnp.concatenate([a_high, a_high, a_low], axis=0)
    b = jnp.concatenate([b_high, b_low, b_high], axis=0)
    return lax.dot_general(a, b, TN, preferred_element_type=jnp.float32)


def partial_kernel(dims, below, above, *refs):
    parts, local_rows, slots, side, meta_rows = dims
    per = slots // 3
    data = local_rows * per * side
    outs, (meta, acc, meta_sems) = refs[:parts], refs[parts:]
    fetches = []
    for index, payload in enumerate((below, above)):
        source = payload.at[pl.ds(data, meta_rows)]
        fetches.append(pltpu.make_async_copy(source, meta.at[index], meta_sems.at[index]))
        fetches[-1].start()
    acc[...] = jnp.zeros_like(acc)
    for index, (payload, lane) in enumerate(((below, 2 * per), (above, 0))):
        fetches[index].wait()
        for line in range(local_rows * per):
            first = line // per * per
            blocks = [payload[t * side : (t + 1) * side, :] for t in range(first, first + per)]
            result = multiplied(payload[line * side : (line + 1) * side, :], blocks)
            dest = meta[index, line, slots].astype(jnp.int32)
            for t in range(per):
                target = meta[index, line, lane + t].astype(jnp.int32)
                place = jnp.minimum(target - per, per)
                acc[dest, place] += result[:, t * side : (t + 1) * side]
    for part in range(parts):
        for row in range(local_rows):
            for t in range(per):
                start = (row * per + t) * side
                outs[part][start : start + side, :] = acc[part * local_rows + row, t]


def sums_kernel(dims, plan, *refs):
    offset, parts, local_rows, slots, side, meta_rows, a_at, group_total, first, width = dims
    per = slots // 3
    data = local_rows * per * side
    payloads = [refs[g * parts : (g + 1) * parts] for g in range(group_total)]
    *base, out, meta, listed, acc, meta_sems = refs[group_total * parts :]

    fetches = []
    for part in range(parts):
        source = payloads[a_at][part].at[pl.ds(data, meta_rows)]
        fetches.append(pltpu.make_async_copy(source, meta.at[part], meta_sems.at[part]))
        fetches[-1].start()
    acc[...] = jnp.zeros_like(acc)

    for part in range(parts):
        fetches[part].wait()
        count = jnp.int32(0)
        for line in range(local_rows * per):
            dest = meta[part, line, slots].astype(jnp.int32) - (offset + part) * local_rows
            listed[0, count] = line
            listed[1, count] = line // per
            listed[2, count] = dest
            mine = (dest >= 0) & (dest < local_rows)
            count = count + mine.astype(jnp.int32)

        def multiply(item, _, part=part):
            line, row, dest = listed[0, item], listed[1, item], listed[2, item]
            start = pl.multiple_of(line * side, side)
            a = payloads[a_at][part][pl.ds(start, side), :]
            for group, lane in plan:
                blocks = []
                for t in range(per):
                    start = pl.multiple_of((row * per + t) * side, side)
                    blocks.append(payloads[group][part][pl.ds(start, side), :])
                result = multiplied(a, blocks)
                for t in range(per):
                    target = meta[part, line, lane + t].astype(jnp.int32)
                    place = jnp.minimum(target - first, width)
                    acc[dest, place] += result[:, t * side : (t + 1) * side]
            return 0

        lax.fori_loop(0, count, multiply, 0)
    for row in range(local_rows):
        for t in range(width):
            if base and width == slots:
                out[row, t] = base[0][row, t] - acc[row, t]
            elif width == slots:
                start = (row * per + t % per) * side
                mine = payloads[t // per][0][start : start + side, :]
                out[row, t] = 2.0 * mine - acc[row, t]
            else:
                start = (row * width + t) * side
                lines = slice(start, start + side)
                out[lines, :] = base[0][lines, :] + acc[row, t] if base else acc[row, t]


def finish_kernel(first, base, *refs):
    groups, (out, result, sems) = refs[:-3], refs[-3:]
    local_rows, slots, side, _ = base.shape
    per = slots // 3
    last = first + per * len(groups)
    copies = []
    for row in range(local_rows):
        for index, group in enumerate(groups):
            for slot in range(per):
                start = (row * per + slot) * side
                total = sum(one[start : start + side, :] for one in group)
                at = first + index * per + slot
                result[row, at - first] = base[row, at] - total
        dest = out.at[row, pl.ds(first, last - first)]
        copies.append(pltpu.make_async_copy(result.at[row], dest, sems.at[row]))
        copies[-1].start()
    for copy in copies:
        copy.wait()


def shards(density, block_cols, targets):
    local_rows, slots, side, _ = density.shape
    per = slots // 3
    parts = lax.axis_size("inner")
    strip_rows = local_rows * parts
    meta_rows = local_rows * per + -(local_rows * per) % 8
    used_rows = local_rows * per * side + meta_rows
    payload_rows = used_rows + 7
    in_hbm = pl.BlockSpec(memory_space=pltpu.HBM)
    scalars = pl.BlockSpec(memory_space=pltpu.SMEM)
    vectors = pl.BlockSpec(memory_space=pltpu.VMEM)

    codes = jnp.concatenate([jnp.transpose(targets, (1, 0, 2)), block_cols[None]], axis=0)
    lower, middle, upper = pl.pallas_call(
        functools.partial(pack_kernel, (local_rows, slots, side, strip_rows, meta_rows)),
        out_shape=[jax.ShapeDtypeStruct((payload_rows, side), jnp.float32)] * 3,
        in_specs=[in_hbm, vectors, scalars],
        out_specs=[vectors] * 3,
        scratch_shapes=[
            pltpu.SemaphoreType.DMA((3, local_rows)),
        ],
        compiler_params=pltpu.CompilerParams(vmem_limit_bytes=52 << 20),
        name="pack",
    )(
        density.reshape(-1, side),
        codes,
        lax.axis_index("inner").reshape(1),
    )

    lines = local_rows * per * side

    def sums(groups, a_at, plan, first, width, offset=0, base=(), spare=0):
        held = len(groups[0])
        dims = (offset, held, local_rows, slots, side, meta_rows, a_at, len(groups), first, width)
        return pl.pallas_call(
            functools.partial(sums_kernel, dims, plan),
            out_shape=jax.ShapeDtypeStruct(
                (lines + spare, side) if width == per else density.shape,
                jnp.float32,
            ),
            in_specs=[vectors] * (held * len(groups) + len(base)),
            out_specs=vectors,
            scratch_shapes=[
                pltpu.SMEM((held, meta_rows, side), jnp.float32),
                pltpu.SMEM((3, local_rows * per + 1), jnp.int32),
                pltpu.VMEM((local_rows, width + 1, side, side), jnp.float32),
                pltpu.SemaphoreType.DMA((held,)),
            ],
            compiler_params=pltpu.CompilerParams(vmem_limit_bytes=16 << 20),
            cost_estimate=pl.CostEstimate(flops=1, bytes_accessed=1, transcendentals=0),
            name="sums",
        )(*[payload for group in groups for payload in group], *base)

    def strip_sums(groups, a_at, plan, first, spare):
        early = parts // 2 + 1
        total = sums([group[:early] for group in groups], a_at, plan, first, per, spare=spare)
        if parts > early:
            rest = [group[early:] for group in groups]
            total = sums(rest, a_at, plan, first, per, early, [total], spare)
        return total

    def spread(far):
        return [one for value in far for one in halves(value[:used_rows])]

    def tied(values, *after):
        return list(lax.optimization_barrier((*values, *after)))[: len(values)]

    def partials(below, above):
        return pl.pallas_call(
            functools.partial(partial_kernel, (parts, local_rows, slots, side, meta_rows)),
            out_shape=[
                jax.ShapeDtypeStruct((lines + 10, side), jnp.float32)
            ] * parts,
            in_specs=[vectors] * 2,
            out_specs=[vectors] * parts,
            scratch_shapes=[
                pltpu.SMEM((2, meta_rows, side), jnp.float32),
                pltpu.VMEM((strip_rows, per + 1, side, side), jnp.float32),
                pltpu.SemaphoreType.DMA((2,)),
            ],
            compiler_params=pltpu.CompilerParams(vmem_limit_bytes=16 << 20),
            cost_estimate=pl.CostEstimate(flops=1, bytes_accessed=1, transcendentals=0),
            name="partials",
        )(below, above)

    own_plan = ((0, 0), (1, per), (2, 2 * per))
    below, above = shifted(upper, 1), shifted(lower, -1)
    lowers, middles, uppers = halves(lower), halves(middle), halves(upper)
    far_middle = across(middle)
    base = sums([lowers, middles, uppers], 1, own_plan, 0, slots)

    far_upper = across(upper, [base])
    far_middles = spread(far_middle)
    far_lower = across(lower, far_middles)
    all_middles = middles + far_middles
    far_uppers = spread(tied(far_upper, below, above))
    below_next = strip_sums([uppers + far_uppers, all_middles], 0, ((1, per),), 0, 22)
    to_below_next = shifted_aslant(below_next, 1)

    shares = dict(enumerate(partials(*tied([below, above], below_next))))
    for bit in [1 << i for i in range(20) if (1 << i) < parts // 2]:
        shares = {
            distance: share + swapped(shares[distance ^ bit], bit)
            for distance, share in shares.items()
            if not distance & bit
        }
    far_share = across(shares[parts // 2], [below_next, shares[0]]) if parts > 1 else []
    far_lowers = spread(tied(far_lower, below_next)) if far_lower else []
    above_next = strip_sums([lowers + far_lowers, all_middles], 0, ((1, per),), 2 * per, 9)
    to_above_next = shifted(above_next, -1)
    if far_lowers:
        near = len(lowers)
        groups = [far_lowers, far_middles, far_uppers]
        base = sums(groups, 1, own_plan, 0, slots, near, [base])
        to_below_next = swapped(to_below_next[:lines], 1)
    middle_shares = [shares[0], *far_share]
    def finish(first, groups, result=()):
        counts = [len(group) for group in groups]
        flat = [one for group in groups for one in group]

        def kernel(base, *refs):
            ends = [sum(counts[: i + 1]) for i in range(len(counts))]
            grouped = [refs[end - count : end] for end, count in zip(ends, counts)]
            finish_kernel(first, base, *grouped, *refs[-3:])

        return pl.pallas_call(
            kernel,
            out_shape=jax.ShapeDtypeStruct(density.shape, jnp.float32),
            in_specs=[vectors] * (1 + len(flat)) + [in_hbm] * len(result),
            out_specs=in_hbm,
            scratch_shapes=[
                pltpu.VMEM((local_rows, per * len(groups), side, side), jnp.float32),
                pltpu.SemaphoreType.DMA((local_rows,)),
            ],
            input_output_aliases={1 + len(flat): 0} if result else {},
            compiler_params=pltpu.CompilerParams(vmem_limit_bytes=16 << 20),
            cost_estimate=pl.CostEstimate(flops=1, bytes_accessed=1, transcendentals=0),
            name="finish",
        )(base, *flat, *result)

    purified = finish(0, [[to_below_next], middle_shares])
    return finish(2 * per, [[to_above_next]], [purified])


def solution(mesh):
    return jax.shard_map(
        shards,
        mesh=mesh,
        in_specs=(
            P(("blk", "inner"), None, None, None),
            P(("blk", "inner"), None),
            P(("blk", "inner"), None, None),
        ),
        out_specs=P(("blk", "inner"), None, None, None),
        check_vma=False,
    )
```

```python
import functools

import jax
import jax.numpy as jnp
from jax import lax
from jax.experimental import pallas as pl
from jax.experimental.pallas import tpu as pltpu
from jax.sharding import PartitionSpec as P

TN = (((0,), (0,)), ((), ()))


def shifted(value, steps):
    count = lax.axis_size("blk")
    pairs = [(source, (source + steps) % count) for source in range(count)]
    return lax.ppermute(value, "blk", pairs)


def shifted_aslant(value, steps):
    count, width = lax.axis_size("blk"), lax.axis_size("inner")
    if width == 1:
        return shifted(value, steps)
    pairs = [
        (s * width + i, (s + steps) % count * width + (i ^ 1))
        for s in range(count)
        for i in range(width)
    ]
    return lax.ppermute(value, ("blk", "inner"), pairs)


def swapped(value, distance):
    count = lax.axis_size("inner")
    return lax.ppermute(value, "inner", [(i, i ^ distance) for i in range(count)])


def halves(value):
    held = [value]
    for bit in [1 << i for i in range(20) if (1 << i) < lax.axis_size("inner") // 2]:
        held = held + [swapped(one, bit) for one in held]
    return held


def across(value, after=()):
    count = lax.axis_size("inner")
    value = lax.optimization_barrier((value, *after))[0] if after else value
    return [swapped(value, count // 2)] if count > 1 else []


def parted(value, size):
    if size & (size - 1) == 0:
        return value >> (size.bit_length() - 1), value & (size - 1)
    return lax.div(value, size), lax.rem(value, size)


def pack_kernel(dims, density, codes, inner, *refs):
    local_rows, slots, side, strip_rows, meta_rows = dims
    per = slots // 3
    data = local_rows * per * side
    outs, sems = refs[:3], refs[3]
    copies = []
    for group in (0, 2, 1):
        for row in range(local_rows):
            source = density.at[pl.ds((row * slots + group * per) * side, per * side)]
            dest = outs[group].at[pl.ds(row * per * side, per * side)]
            copies.append(pltpu.make_async_copy(source, dest, sems.at[group, row]))
            copies[-1].start()
    for group in (0, 2, 1):
        outs[group][data : data + meta_rows, :] = jnp.zeros((meta_rows, side), jnp.float32)
    lanes = lax.broadcasted_iota(jnp.int32, (local_rows, slots), 1)
    owner, place = parted(parted(codes[slots], strip_rows)[1], local_rows)
    dests = ((owner ^ inner[0]) * local_rows + place).astype(jnp.float32)
    for group in (0, 2, 1):
        for slot in range(per):
            chosen = codes[group * per + slot].astype(jnp.float32)
            mine = jnp.where(lanes == group * per + slot, dests, 0.0)
            dest = jnp.sum(mine, axis=1, keepdims=True)
            for row in range(local_rows):
                at = data + row * per + slot
                outs[group][at : at + 1, :slots] = chosen[row : row + 1]
                outs[group][at : at + 1, slots : slots + 1] = dest[row : row + 1]
    for copy in copies:
        copy.wait()


def cut(block):
    high = block.astype(jnp.bfloat16)
    return high, (block - high.astype(jnp.float32)).astype(jnp.bfloat16)


def multiplied(a, blocks):
    a_high, a_low = cut(a)
    b_high, b_low = cut(jnp.concatenate(blocks, axis=1))
    a = jnp.concatenate([a_high, a_high, a_low], axis=0)
    b = jnp.concatenate([b_high, b_low, b_high], axis=0)
    return lax.dot_general(a, b, TN, preferred_element_type=jnp.float32)


def partial_kernel(dims, below, above, *refs):
    parts, local_rows, slots, side, meta_rows = dims
    per = slots // 3
    data = local_rows * per * side
    outs, (meta, acc, meta_sems) = refs[:parts], refs[parts:]
    fetches = []
    for index, payload in enumerate((below, above)):
        source = payload.at[pl.ds(data, meta_rows)]
        fetches.append(pltpu.make_async_copy(source, meta.at[index], meta_sems.at[index]))
        fetches[-1].start()
    acc[...] = jnp.zeros_like(acc)
    for index, (payload, lane) in enumerate(((below, 2 * per), (above, 0))):
        fetches[index].wait()
        for line in range(local_rows * per):
            first = line // per * per
            blocks = [payload[t * side : (t + 1) * side, :] for t in range(first, first + per)]
            result = multiplied(payload[line * side : (line + 1) * side, :], blocks)
            dest = meta[index, line, slots].astype(jnp.int32)
            for t in range(per):
                target = meta[index, line, lane + t].astype(jnp.int32)
                place = jnp.minimum(target - per, per)
                acc[dest, place] += result[:, t * side : (t + 1) * side]
    for part in range(parts):
        for row in range(local_rows):
            for t in range(per):
                start = (row * per + t) * side
                outs[part][start : start + side, :] = acc[part * local_rows + row, t]


def sums_kernel(dims, plan, *refs):
    offset, parts, local_rows, slots, side, meta_rows, a_at, group_total, first, width = dims
    per = slots // 3
    data = local_rows * per * side
    payloads = [refs[g * parts : (g + 1) * parts] for g in range(group_total)]
    *base, out, meta, listed, acc, meta_sems = refs[group_total * parts :]

    fetches = []
    for part in range(parts):
        source = payloads[a_at][part].at[pl.ds(data, meta_rows)]
        fetches.append(pltpu.make_async_copy(source, meta.at[part], meta_sems.at[part]))
        fetches[-1].start()
    acc[...] = jnp.zeros_like(acc)

    for part in range(parts):
        fetches[part].wait()
        count = jnp.int32(0)
        for line in range(local_rows * per):
            dest = meta[part, line, slots].astype(jnp.int32) - (offset + part) * local_rows
            listed[0, count] = line
            listed[1, count] = line // per
            listed[2, count] = dest
            mine = (dest >= 0) & (dest < local_rows)
            count = count + mine.astype(jnp.int32)

        def multiply(item, _, part=part):
            line, row, dest = listed[0, item], listed[1, item], listed[2, item]
            start = pl.multiple_of(line * side, side)
            a = payloads[a_at][part][pl.ds(start, side), :]
            for group, lane in plan:
                blocks = []
                for t in range(per):
                    start = pl.multiple_of((row * per + t) * side, side)
                    blocks.append(payloads[group][part][pl.ds(start, side), :])
                result = multiplied(a, blocks)
                for t in range(per):
                    target = meta[part, line, lane + t].astype(jnp.int32)
                    place = jnp.minimum(target - first, width)
                    acc[dest, place] += result[:, t * side : (t + 1) * side]
            return 0

        lax.fori_loop(0, count, multiply, 0)
    for row in range(local_rows):
        for t in range(width):
            if base and width == slots:
                out[row, t] = base[0][row, t] - acc[row, t]
            elif width == slots:
                start = (row * per + t % per) * side
                mine = payloads[t // per][0][start : start + side, :]
                out[row, t] = 2.0 * mine - acc[row, t]
            else:
                start = (row * width + t) * side
                lines = slice(start, start + side)
                out[lines, :] = base[0][lines, :] + acc[row, t] if base else acc[row, t]


def finish_kernel(first, base, *refs):
    groups, (out, result, sems) = refs[:-3], refs[-3:]
    local_rows, slots, side, _ = base.shape
    per = slots // 3
    last = first + per * len(groups)
    copies = []
    for row in range(local_rows):
        for index, group in enumerate(groups):
            for slot in range(per):
                start = (row * per + slot) * side
                total = sum(one[start : start + side, :] for one in group)
                at = first + index * per + slot
                result[row, at - first] = base[row, at] - total
        dest = out.at[row, pl.ds(first, last - first)]
        copies.append(pltpu.make_async_copy(result.at[row], dest, sems.at[row]))
        copies[-1].start()
    for copy in copies:
        copy.wait()


def shards(density, block_cols, targets):
    local_rows, slots, side, _ = density.shape
    per = slots // 3
    parts = lax.axis_size("inner")
    strip_rows = local_rows * parts
    meta_rows = local_rows * per + -(local_rows * per) % 8
    used_rows = local_rows * per * side + meta_rows
    payload_rows = used_rows + 7
    in_hbm = pl.BlockSpec(memory_space=pltpu.HBM)
    scalars = pl.BlockSpec(memory_space=pltpu.SMEM)
    vectors = pl.BlockSpec(memory_space=pltpu.VMEM)

    codes = jnp.concatenate([jnp.transpose(targets, (1, 0, 2)), block_cols[None]], axis=0)
    lower, middle, upper = pl.pallas_call(
        functools.partial(pack_kernel, (local_rows, slots, side, strip_rows, meta_rows)),
        out_shape=[jax.ShapeDtypeStruct((payload_rows, side), jnp.float32)] * 3,
        in_specs=[in_hbm, vectors, scalars],
        out_specs=[vectors] * 3,
        scratch_shapes=[
            pltpu.SemaphoreType.DMA((3, local_rows)),
        ],
        compiler_params=pltpu.CompilerParams(vmem_limit_bytes=52 << 20),
        name="pack",
    )(
        density.reshape(-1, side),
        codes,
        lax.axis_index("inner").reshape(1),
    )

    lines = local_rows * per * side

    def sums(groups, a_at, plan, first, width, offset=0, base=(), spare=0):
        held = len(groups[0])
        dims = (offset, held, local_rows, slots, side, meta_rows, a_at, len(groups), first, width)
        return pl.pallas_call(
            functools.partial(sums_kernel, dims, plan),
            out_shape=jax.ShapeDtypeStruct(
                (lines + spare, side) if width == per else density.shape,
                jnp.float32,
            ),
            in_specs=[vectors] * (held * len(groups) + len(base)),
            out_specs=vectors,
            scratch_shapes=[
                pltpu.SMEM((held, meta_rows, side), jnp.float32),
                pltpu.SMEM((3, local_rows * per + 1), jnp.int32),
                pltpu.VMEM((local_rows, width + 1, side, side), jnp.float32),
                pltpu.SemaphoreType.DMA((held,)),
            ],
            compiler_params=pltpu.CompilerParams(vmem_limit_bytes=16 << 20),
            cost_estimate=pl.CostEstimate(flops=1, bytes_accessed=1, transcendentals=0),
            name="sums",
        )(*[payload for group in groups for payload in group], *base)

    def strip_sums(groups, a_at, plan, first, spare):
        early = parts // 2 + 1
        begun = total = sums([group[:early] for group in groups], a_at, plan, first, per, spare=spare)
        if parts > early:
            rest = [group[early:] for group in groups]
            total = sums(rest, a_at, plan, first, per, early, [total], spare)
        return total, begun

    def spread(far):
        return [one for value in far for one in halves(value[:used_rows])]

    def tied(values, *after):
        return list(lax.optimization_barrier((*values, *after)))[: len(values)]

    def partials(below, above):
        return pl.pallas_call(
            functools.partial(partial_kernel, (parts, local_rows, slots, side, meta_rows)),
            out_shape=[
                jax.ShapeDtypeStruct((lines + 10, side), jnp.float32)
            ] * parts,
            in_specs=[vectors] * 2,
            out_specs=[vectors] * parts,
            scratch_shapes=[
                pltpu.SMEM((2, meta_rows, side), jnp.float32),
                pltpu.VMEM((strip_rows, per + 1, side, side), jnp.float32),
                pltpu.SemaphoreType.DMA((2,)),
            ],
            compiler_params=pltpu.CompilerParams(vmem_limit_bytes=16 << 20),
            cost_estimate=pl.CostEstimate(flops=1, bytes_accessed=1, transcendentals=0),
            name="partials",
        )(below, above)

    own_plan = ((0, 0), (1, per), (2, 2 * per))
    below, above = shifted(upper, 1), shifted(lower, -1)
    lowers, middles, uppers = halves(lower), halves(middle), halves(upper)
    far_middle = across(middle)
    base = sums([lowers, middles, uppers], 1, own_plan, 0, slots)

    far_upper = across(upper, [base])
    far_middles = spread(far_middle)
    far_lower = across(lower, far_middles)
    all_middles = middles + far_middles
    far_uppers = spread(tied(far_upper, below, above))
    below_next, _ = strip_sums([uppers + far_uppers, all_middles], 0, ((1, per),), 0, 22)
    to_below_next = shifted_aslant(below_next, 1)

    shares = dict(enumerate(partials(*tied([below, above], below_next))))
    for bit in [1 << i for i in range(20) if (1 << i) < parts // 2]:
        shares = {
            distance: share + swapped(shares[distance ^ bit], bit)
            for distance, share in shares.items()
            if not distance & bit
        }
    far_lowers = spread(tied(far_lower, below_next)) if far_lower else []
    above_next, begun = strip_sums([lowers + far_lowers, all_middles], 0, ((1, per),), 2 * per, 9)
    far_share = across(shares[parts // 2], [begun, shares[0]]) if parts > 1 else []
    to_above_next = shifted(above_next, -1)
    if far_lowers:
        near = len(lowers)
        groups = [far_lowers, far_middles, far_uppers]
        base = sums(groups, 1, own_plan, 0, slots, near, [base])
        to_below_next = swapped(to_below_next[:lines], 1)
    middle_shares = [shares[0], *far_share]
    def finish(first, groups, result=()):
        counts = [len(group) for group in groups]
        flat = [one for group in groups for one in group]

        def kernel(base, *refs):
            ends = [sum(counts[: i + 1]) for i in range(len(counts))]
            grouped = [refs[end - count : end] for end, count in zip(ends, counts)]
            finish_kernel(first, base, *grouped, *refs[-3:])

        return pl.pallas_call(
            kernel,
            out_shape=jax.ShapeDtypeStruct(density.shape, jnp.float32),
            in_specs=[vectors] * (1 + len(flat)) + [in_hbm] * len(result),
            out_specs=in_hbm,
            scratch_shapes=[
                pltpu.VMEM((local_rows, per * len(groups), side, side), jnp.float32),
                pltpu.SemaphoreType.DMA((local_rows,)),
            ],
            input_output_aliases={1 + len(flat): 0} if result else {},
            compiler_params=pltpu.CompilerParams(vmem_limit_bytes=16 << 20),
            cost_estimate=pl.CostEstimate(flops=1, bytes_accessed=1, transcendentals=0),
            name="finish",
        )(base, *flat, *result)

    purified = finish(0, [[to_below_next], middle_shares])
    return finish(2 * per, [[to_above_next]], [purified])


def solution(mesh):
    return jax.shard_map(
        shards,
        mesh=mesh,
        in_specs=(
            P(("blk", "inner"), None, None, None),
            P(("blk", "inner"), None),
            P(("blk", "inner"), None, None),
        ),
        out_specs=P(("blk", "inner"), None, None, None),
        check_vma=False,
    )
```

```python
import functools

import jax
import jax.numpy as jnp
from jax import lax
from jax.experimental import pallas as pl
from jax.experimental.pallas import tpu as pltpu
from jax.sharding import PartitionSpec as P

TN = (((0,), (0,)), ((), ()))


def shifted(value, steps):
    count = lax.axis_size("blk")
    pairs = [(source, (source + steps) % count) for source in range(count)]
    return lax.ppermute(value, "blk", pairs)


def shifted_aslant(value, steps):
    count, width = lax.axis_size("blk"), lax.axis_size("inner")
    if width == 1:
        return shifted(value, steps)
    pairs = [
        (s * width + i, (s + steps) % count * width + (i ^ 1))
        for s in range(count)
        for i in range(width)
    ]
    return lax.ppermute(value, ("blk", "inner"), pairs)


def swapped(value, distance):
    count = lax.axis_size("inner")
    return lax.ppermute(value, "inner", [(i, i ^ distance) for i in range(count)])


def halves(value):
    held = [value]
    for bit in [1 << i for i in range(20) if (1 << i) < lax.axis_size("inner") // 2]:
        held = held + [swapped(one, bit) for one in held]
    return held


def across(value, after=()):
    count = lax.axis_size("inner")
    value = lax.optimization_barrier((value, *after))[0] if after else value
    return [swapped(value, count // 2)] if count > 1 else []


def parted(value, size):
    if size & (size - 1) == 0:
        return value >> (size.bit_length() - 1), value & (size - 1)
    return lax.div(value, size), lax.rem(value, size)


def pack_kernel(dims, density, codes, inner, *refs):
    local_rows, slots, side, strip_rows, meta_rows = dims
    per = slots // 3
    data = local_rows * per * side
    outs, sems = refs[:3], refs[3]
    copies = []
    for group in (0, 2, 1):
        for row in range(local_rows):
            source = density.at[pl.ds((row * slots + group * per) * side, per * side)]
            dest = outs[group].at[pl.ds(row * per * side, per * side)]
            copies.append(pltpu.make_async_copy(source, dest, sems.at[group, row]))
            copies[-1].start()
    for group in (0, 2, 1):
        outs[group][data : data + meta_rows, :] = jnp.zeros((meta_rows, side), jnp.float32)
    lanes = lax.broadcasted_iota(jnp.int32, (local_rows, slots), 1)
    owner, place = parted(parted(codes[slots], strip_rows)[1], local_rows)
    dests = ((owner ^ inner[0]) * local_rows + place).astype(jnp.float32)
    for group in (0, 2, 1):
        for slot in range(per):
            chosen = codes[group * per + slot].astype(jnp.float32)
            mine = jnp.where(lanes == group * per + slot, dests, 0.0)
            dest = jnp.sum(mine, axis=1, keepdims=True)
            for row in range(local_rows):
                at = data + row * per + slot
                outs[group][at : at + 1, :slots] = chosen[row : row + 1]
                outs[group][at : at + 1, slots : slots + 1] = dest[row : row + 1]
    for copy in copies:
        copy.wait()


def cut(block):
    high = block.astype(jnp.bfloat16)
    return high, (block - high.astype(jnp.float32)).astype(jnp.bfloat16)


def multiplied(a, blocks):
    a_high, a_low = cut(a)
    b_high, b_low = cut(jnp.concatenate(blocks, axis=1))
    a = jnp.concatenate([a_high, a_high, a_low], axis=0)
    b = jnp.concatenate([b_high, b_low, b_high], axis=0)
    return lax.dot_general(a, b, TN, preferred_element_type=jnp.float32)


def partial_kernel(dims, below, above, *refs):
    parts, local_rows, slots, side, meta_rows = dims
    per = slots // 3
    data = local_rows * per * side
    outs, (meta, acc, meta_sems) = refs[:parts], refs[parts:]
    fetches = []
    for index, payload in enumerate((below, above)):
        source = payload.at[pl.ds(data, meta_rows)]
        fetches.append(pltpu.make_async_copy(source, meta.at[index], meta_sems.at[index]))
        fetches[-1].start()
    acc[...] = jnp.zeros_like(acc)
    for index, (payload, lane) in enumerate(((below, 2 * per), (above, 0))):
        fetches[index].wait()
        for line in range(local_rows * per):
            first = line // per * per
            blocks = [payload[t * side : (t + 1) * side, :] for t in range(first, first + per)]
            result = multiplied(payload[line * side : (line + 1) * side, :], blocks)
            dest = meta[index, line, slots].astype(jnp.int32)
            for t in range(per):
                target = meta[index, line, lane + t].astype(jnp.int32)
                place = jnp.minimum(target - per, per)
                acc[dest, place] += result[:, t * side : (t + 1) * side]
    for part in range(parts):
        for row in range(local_rows):
            for t in range(per):
                start = (row * per + t) * side
                outs[part][start : start + side, :] = acc[part * local_rows + row, t]


def sums_kernel(dims, plan, *refs):
    offset, parts, local_rows, slots, side, meta_rows, a_at, group_total, first, width = dims
    per = slots // 3
    data = local_rows * per * side
    payloads = [refs[g * parts : (g + 1) * parts] for g in range(group_total)]
    *base, out, meta, listed, acc, meta_sems = refs[group_total * parts :]

    fetches = []
    for part in range(parts):
        source = payloads[a_at][part].at[pl.ds(data, meta_rows)]
        fetches.append(pltpu.make_async_copy(source, meta.at[part], meta_sems.at[part]))
        fetches[-1].start()
    acc[...] = jnp.zeros_like(acc)

    for part in range(parts):
        fetches[part].wait()
        count = jnp.int32(0)
        for line in range(local_rows * per):
            dest = meta[part, line, slots].astype(jnp.int32) - (offset + part) * local_rows
            listed[0, count] = line
            listed[1, count] = line // per
            listed[2, count] = dest
            mine = (dest >= 0) & (dest < local_rows)
            count = count + mine.astype(jnp.int32)

        def multiply(item, _, part=part):
            line, row, dest = listed[0, item], listed[1, item], listed[2, item]
            start = pl.multiple_of(line * side, side)
            a = payloads[a_at][part][pl.ds(start, side), :]
            for group, lane in plan:
                blocks = []
                for t in range(per):
                    start = pl.multiple_of((row * per + t) * side, side)
                    blocks.append(payloads[group][part][pl.ds(start, side), :])
                result = multiplied(a, blocks)
                for t in range(per):
                    target = meta[part, line, lane + t].astype(jnp.int32)
                    place = jnp.minimum(target - first, width)
                    acc[dest, place] += result[:, t * side : (t + 1) * side]
            return 0

        lax.fori_loop(0, count, multiply, 0)
    for row in range(local_rows):
        for t in range(width):
            if base and width == slots:
                out[row, t] = base[0][row, t] - acc[row, t]
            elif width == slots:
                start = (row * per + t % per) * side
                mine = payloads[t // per][0][start : start + side, :]
                out[row, t] = 2.0 * mine - acc[row, t]
            else:
                start = (row * width + t) * side
                lines = slice(start, start + side)
                out[lines, :] = base[0][lines, :] + acc[row, t] if base else acc[row, t]


def finish_kernel(first, base, *refs):
    groups, (out, result, sems) = refs[:-3], refs[-3:]
    local_rows, slots, side, _ = base.shape
    per = slots // 3
    last = first + per * len(groups)
    copies = []
    for row in range(local_rows):
        for index, group in enumerate(groups):
            for slot in range(per):
                start = (row * per + slot) * side
                total = sum(one[start : start + side, :] for one in group)
                at = first + index * per + slot
                result[row, at - first] = base[row, at] - total
        dest = out.at[row, pl.ds(first, last - first)]
        copies.append(pltpu.make_async_copy(result.at[row], dest, sems.at[row]))
        copies[-1].start()
    for copy in copies:
        copy.wait()


def shards(density, block_cols, targets):
    local_rows, slots, side, _ = density.shape
    per = slots // 3
    parts = lax.axis_size("inner")
    strip_rows = local_rows * parts
    meta_rows = local_rows * per + -(local_rows * per) % 8
    used_rows = local_rows * per * side + meta_rows
    payload_rows = used_rows + 7
    in_hbm = pl.BlockSpec(memory_space=pltpu.HBM)
    scalars = pl.BlockSpec(memory_space=pltpu.SMEM)
    vectors = pl.BlockSpec(memory_space=pltpu.VMEM)

    codes = jnp.concatenate([jnp.transpose(targets, (1, 0, 2)), block_cols[None]], axis=0)
    lower, middle, upper = pl.pallas_call(
        functools.partial(pack_kernel, (local_rows, slots, side, strip_rows, meta_rows)),
        out_shape=[jax.ShapeDtypeStruct((payload_rows, side), jnp.float32)] * 3,
        in_specs=[in_hbm, vectors, scalars],
        out_specs=[vectors] * 3,
        scratch_shapes=[
            pltpu.SemaphoreType.DMA((3, local_rows)),
        ],
        compiler_params=pltpu.CompilerParams(vmem_limit_bytes=52 << 20),
        name="pack",
    )(
        density.reshape(-1, side),
        codes,
        lax.axis_index("inner").reshape(1),
    )

    lines = local_rows * per * side

    def sums(groups, a_at, plan, first, width, offset=0, base=(), spare=0):
        held = len(groups[0])
        dims = (offset, held, local_rows, slots, side, meta_rows, a_at, len(groups), first, width)
        return pl.pallas_call(
            functools.partial(sums_kernel, dims, plan),
            out_shape=jax.ShapeDtypeStruct(
                (lines + spare, side) if width == per else density.shape,
                jnp.float32,
            ),
            in_specs=[vectors] * (held * len(groups) + len(base)),
            out_specs=vectors,
            scratch_shapes=[
                pltpu.SMEM((held, meta_rows, side), jnp.float32),
                pltpu.SMEM((3, local_rows * per + 1), jnp.int32),
                pltpu.VMEM((local_rows, width + 1, side, side), jnp.float32),
                pltpu.SemaphoreType.DMA((held,)),
            ],
            compiler_params=pltpu.CompilerParams(vmem_limit_bytes=16 << 20),
            cost_estimate=pl.CostEstimate(flops=1, bytes_accessed=1, transcendentals=0),
            name="sums",
        )(*[payload for group in groups for payload in group], *base)

    def strip_sums(groups, a_at, plan, first, spare):
        early = parts // 2 + 1
        begun = total = sums([group[:early] for group in groups], a_at, plan, first, per, spare=spare)
        if parts > early:
            rest = [group[early:] for group in groups]
            total = sums(rest, a_at, plan, first, per, early, [total], spare)
        return total, begun

    def spread(far):
        return [one for value in far for one in halves(value[:used_rows])]

    def tied(values, *after):
        return list(lax.optimization_barrier((*values, *after)))[: len(values)]

    def partials(below, above):
        return pl.pallas_call(
            functools.partial(partial_kernel, (parts, local_rows, slots, side, meta_rows)),
            out_shape=[
                jax.ShapeDtypeStruct((lines + 10, side), jnp.float32)
            ] * parts,
            in_specs=[vectors] * 2,
            out_specs=[vectors] * parts,
            scratch_shapes=[
                pltpu.SMEM((2, meta_rows, side), jnp.float32),
                pltpu.VMEM((strip_rows, per + 1, side, side), jnp.float32),
                pltpu.SemaphoreType.DMA((2,)),
            ],
            compiler_params=pltpu.CompilerParams(vmem_limit_bytes=16 << 20),
            cost_estimate=pl.CostEstimate(flops=1, bytes_accessed=1, transcendentals=0),
            name="partials",
        )(below, above)

    own_plan = ((0, 0), (1, per), (2, 2 * per))
    below, above = shifted(upper, 1), shifted(lower, -1)
    lowers, middles, uppers = halves(lower), halves(middle), halves(upper)
    far_middle = across(middle)
    base = sums([lowers, middles, uppers], 1, own_plan, 0, slots)

    far_upper = across(upper, [base])
    far_middles = spread(far_middle)
    far_lower = across(lower, far_middles)
    all_middles = middles + far_middles
    far_uppers = spread(tied(far_upper, below, above))
    below_next, _ = strip_sums([uppers + far_uppers, all_middles], 0, ((1, per),), 0, 22)
    to_below_next = shifted_aslant(below_next, 1)

    shares = dict(enumerate(partials(*tied([below, above], below_next))))
    for bit in [1 << i for i in range(20) if (1 << i) < parts // 2]:
        shares = {
            distance: share + swapped(shares[distance ^ bit], bit)
            for distance, share in shares.items()
            if not distance & bit
        }
    far_lowers = spread(tied(far_lower, below_next)) if far_lower else []
    above_next, begun = strip_sums([lowers + far_lowers, all_middles], 0, ((1, per),), 2 * per, 9)
    far_share = across(shares[parts // 2], [begun, shares[0]]) if parts > 1 else []
    to_above_next = shifted(above_next, -1)
    if far_lowers:
        near = len(lowers)
        groups = [far_lowers, far_middles, far_uppers]
        base = sums(groups, 1, own_plan, 0, slots, near, [base])
        to_below_next = swapped(tied([to_below_next], base)[0][:lines], 1)
    middle_shares = [shares[0], *far_share]
    def finish(first, groups, result=()):
        counts = [len(group) for group in groups]
        flat = [one for group in groups for one in group]

        def kernel(base, *refs):
            ends = [sum(counts[: i + 1]) for i in range(len(counts))]
            grouped = [refs[end - count : end] for end, count in zip(ends, counts)]
            finish_kernel(first, base, *grouped, *refs[-3:])

        return pl.pallas_call(
            kernel,
            out_shape=jax.ShapeDtypeStruct(density.shape, jnp.float32),
            in_specs=[vectors] * (1 + len(flat)) + [in_hbm] * len(result),
            out_specs=in_hbm,
            scratch_shapes=[
                pltpu.VMEM((local_rows, per * len(groups), side, side), jnp.float32),
                pltpu.SemaphoreType.DMA((local_rows,)),
            ],
            input_output_aliases={1 + len(flat): 0} if result else {},
            compiler_params=pltpu.CompilerParams(vmem_limit_bytes=16 << 20),
            cost_estimate=pl.CostEstimate(flops=1, bytes_accessed=1, transcendentals=0),
            name="finish",
        )(base, *flat, *result)

    purified = finish(0, [[to_below_next], middle_shares])
    return finish(2 * per, [[to_above_next]], [purified])


def solution(mesh):
    return jax.shard_map(
        shards,
        mesh=mesh,
        in_specs=(
            P(("blk", "inner"), None, None, None),
            P(("blk", "inner"), None),
            P(("blk", "inner"), None, None),
        ),
        out_specs=P(("blk", "inner"), None, None, None),
        check_vma=False,
    )
```

```python
import functools

import jax
import jax.numpy as jnp
from jax import lax
from jax.experimental import pallas as pl
from jax.experimental.pallas import tpu as pltpu
from jax.sharding import PartitionSpec as P

TN = (((0,), (0,)), ((), ()))


def shifted(value, steps):
    count = lax.axis_size("blk")
    pairs = [(source, (source + steps) % count) for source in range(count)]
    return lax.ppermute(value, "blk", pairs)


def shifted_aslant(value, steps):
    count, width = lax.axis_size("blk"), lax.axis_size("inner")
    if width == 1:
        return shifted(value, steps)
    pairs = [
        (s * width + i, (s + steps) % count * width + (i ^ 1))
        for s in range(count)
        for i in range(width)
    ]
    return lax.ppermute(value, ("blk", "inner"), pairs)


def swapped(value, distance):
    count = lax.axis_size("inner")
    return lax.ppermute(value, "inner", [(i, i ^ distance) for i in range(count)])


def halves(value):
    held = [value]
    for bit in [1 << i for i in range(20) if (1 << i) < lax.axis_size("inner") // 2]:
        held = held + [swapped(one, bit) for one in held]
    return held


def across(value, after=()):
    count = lax.axis_size("inner")
    value = lax.optimization_barrier((value, *after))[0] if after else value
    return [swapped(value, count // 2)] if count > 1 else []


def parted(value, size):
    if size & (size - 1) == 0:
        return value >> (size.bit_length() - 1), value & (size - 1)
    return lax.div(value, size), lax.rem(value, size)


def pack_kernel(dims, density, codes, inner, *refs):
    local_rows, slots, side, strip_rows, meta_rows = dims
    per = slots // 3
    data = local_rows * per * side
    outs, sems = refs[:3], refs[3]
    copies = []
    for group in (0, 2, 1):
        for row in range(local_rows):
            source = density.at[pl.ds((row * slots + group * per) * side, per * side)]
            dest = outs[group].at[pl.ds(row * per * side, per * side)]
            copies.append(pltpu.make_async_copy(source, dest, sems.at[group, row]))
            copies[-1].start()
    for group in (0, 2, 1):
        outs[group][data : data + meta_rows, :] = jnp.zeros((meta_rows, side), jnp.float32)
    lanes = lax.broadcasted_iota(jnp.int32, (local_rows, slots), 1)
    owner, place = parted(parted(codes[slots], strip_rows)[1], local_rows)
    dests = ((owner ^ inner[0]) * local_rows + place).astype(jnp.float32)
    for group in (0, 2, 1):
        for slot in range(per):
            chosen = codes[group * per + slot].astype(jnp.float32)
            mine = jnp.where(lanes == group * per + slot, dests, 0.0)
            dest = jnp.sum(mine, axis=1, keepdims=True)
            for row in range(local_rows):
                at = data + row * per + slot
                outs[group][at : at + 1, :slots] = chosen[row : row + 1]
                outs[group][at : at + 1, slots : slots + 1] = dest[row : row + 1]
    for copy in copies:
        copy.wait()


def cut(block):
    high = block.astype(jnp.bfloat16)
    return high, (block - high.astype(jnp.float32)).astype(jnp.bfloat16)


def multiplied(a, blocks):
    a_high, a_low = cut(a)
    b_high, b_low = cut(jnp.concatenate(blocks, axis=1))
    a = jnp.concatenate([a_high, a_high, a_low], axis=0)
    b = jnp.concatenate([b_high, b_low, b_high], axis=0)
    return lax.dot_general(a, b, TN, preferred_element_type=jnp.float32)


def partial_kernel(dims, below, above, *refs):
    parts, local_rows, slots, side, meta_rows = dims
    per = slots // 3
    data = local_rows * per * side
    outs, (meta, acc, meta_sems) = refs[:parts], refs[parts:]
    fetches = []
    for index, payload in enumerate((below, above)):
        source = payload.at[pl.ds(data, meta_rows)]
        fetches.append(pltpu.make_async_copy(source, meta.at[index], meta_sems.at[index]))
        fetches[-1].start()
    acc[...] = jnp.zeros_like(acc)
    for index, (payload, lane) in enumerate(((below, 2 * per), (above, 0))):
        fetches[index].wait()
        for line in range(local_rows * per):
            first = line // per * per
            blocks = [payload[t * side : (t + 1) * side, :] for t in range(first, first + per)]
            result = multiplied(payload[line * side : (line + 1) * side, :], blocks)
            dest = meta[index, line, slots].astype(jnp.int32)
            for t in range(per):
                target = meta[index, line, lane + t].astype(jnp.int32)
                place = jnp.minimum(target - per, per)
                acc[dest, place] += result[:, t * side : (t + 1) * side]
    for part in range(parts):
        for row in range(local_rows):
            for t in range(per):
                start = (row * per + t) * side
                outs[part][start : start + side, :] = acc[part * local_rows + row, t]


def sums_kernel(dims, plan, *refs):
    offset, parts, local_rows, slots, side, meta_rows, a_at, group_total, first, width = dims
    per = slots // 3
    data = local_rows * per * side
    payloads = [refs[g * parts : (g + 1) * parts] for g in range(group_total)]
    *base, out, meta, listed, acc, meta_sems = refs[group_total * parts :]

    fetches = []
    for part in range(parts):
        source = payloads[a_at][part].at[pl.ds(data, meta_rows)]
        fetches.append(pltpu.make_async_copy(source, meta.at[part], meta_sems.at[part]))
        fetches[-1].start()
    acc[...] = jnp.zeros_like(acc)

    for part in range(parts):
        fetches[part].wait()
        count = jnp.int32(0)
        for line in range(local_rows * per):
            dest = meta[part, line, slots].astype(jnp.int32) - (offset + part) * local_rows
            listed[0, count] = line
            listed[1, count] = line // per
            listed[2, count] = dest
            mine = (dest >= 0) & (dest < local_rows)
            count = count + mine.astype(jnp.int32)

        def multiply(item, _, part=part):
            line, row, dest = listed[0, item], listed[1, item], listed[2, item]
            start = pl.multiple_of(line * side, side)
            a = payloads[a_at][part][pl.ds(start, side), :]
            for group, lane in plan:
                blocks = []
                for t in range(per):
                    start = pl.multiple_of((row * per + t) * side, side)
                    blocks.append(payloads[group][part][pl.ds(start, side), :])
                result = multiplied(a, blocks)
                for t in range(per):
                    target = meta[part, line, lane + t].astype(jnp.int32)
                    place = jnp.minimum(target - first, width)
                    acc[dest, place] += result[:, t * side : (t + 1) * side]
            return 0

        lax.fori_loop(0, count, multiply, 0)
    for row in range(local_rows):
        for t in range(width):
            if base and width == slots:
                out[row, t] = base[0][row, t] - acc[row, t]
            elif width == slots:
                start = (row * per + t % per) * side
                mine = payloads[t // per][0][start : start + side, :]
                out[row, t] = 2.0 * mine - acc[row, t]
            else:
                start = (row * width + t) * side
                lines = slice(start, start + side)
                out[lines, :] = base[0][lines, :] + acc[row, t] if base else acc[row, t]


def finish_kernel(first, base, *refs):
    groups, (out, result, sems) = refs[:-3], refs[-3:]
    local_rows, slots, side, _ = base.shape
    per = slots // 3
    copies = []
    for row in range(local_rows):
        for index, group in enumerate(groups):
            for slot in range(per):
                start = (row * per + slot) * side
                total = sum(one[start : start + side, :] for one in group)
                at = first + index * per + slot
                result[row, at - first] = base[row, at] - total
                sem = sems.at[row, at - first]
                copies.append(pltpu.make_async_copy(result.at[row, at - first], out.at[row, at], sem))
                copies[-1].start()
    for copy in copies:
        copy.wait()


def shards(density, block_cols, targets):
    local_rows, slots, side, _ = density.shape
    per = slots // 3
    parts = lax.axis_size("inner")
    strip_rows = local_rows * parts
    meta_rows = local_rows * per + -(local_rows * per) % 8
    used_rows = local_rows * per * side + meta_rows
    payload_rows = used_rows + 7
    in_hbm = pl.BlockSpec(memory_space=pltpu.HBM)
    scalars = pl.BlockSpec(memory_space=pltpu.SMEM)
    vectors = pl.BlockSpec(memory_space=pltpu.VMEM)

    codes = jnp.concatenate([jnp.transpose(targets, (1, 0, 2)), block_cols[None]], axis=0)
    lower, middle, upper = pl.pallas_call(
        functools.partial(pack_kernel, (local_rows, slots, side, strip_rows, meta_rows)),
        out_shape=[jax.ShapeDtypeStruct((payload_rows, side), jnp.float32)] * 3,
        in_specs=[in_hbm, vectors, scalars],
        out_specs=[vectors] * 3,
        scratch_shapes=[
            pltpu.SemaphoreType.DMA((3, local_rows)),
        ],
        compiler_params=pltpu.CompilerParams(vmem_limit_bytes=52 << 20),
        name="pack",
    )(
        density.reshape(-1, side),
        codes,
        lax.axis_index("inner").reshape(1),
    )

    lines = local_rows * per * side

    def sums(groups, a_at, plan, first, width, offset=0, base=(), spare=0):
        held = len(groups[0])
        dims = (offset, held, local_rows, slots, side, meta_rows, a_at, len(groups), first, width)
        return pl.pallas_call(
            functools.partial(sums_kernel, dims, plan),
            out_shape=jax.ShapeDtypeStruct(
                (lines + spare, side) if width == per else density.shape,
                jnp.float32,
            ),
            in_specs=[vectors] * (held * len(groups) + len(base)),
            out_specs=vectors,
            scratch_shapes=[
                pltpu.SMEM((held, meta_rows, side), jnp.float32),
                pltpu.SMEM((3, local_rows * per + 1), jnp.int32),
                pltpu.VMEM((local_rows, width + 1, side, side), jnp.float32),
                pltpu.SemaphoreType.DMA((held,)),
            ],
            compiler_params=pltpu.CompilerParams(vmem_limit_bytes=16 << 20),
            cost_estimate=pl.CostEstimate(flops=1, bytes_accessed=1, transcendentals=0),
            name="sums",
        )(*[payload for group in groups for payload in group], *base)

    def strip_sums(groups, a_at, plan, first, spare):
        early = parts // 2 + 1
        begun = total = sums([group[:early] for group in groups], a_at, plan, first, per, spare=spare)
        if parts > early:
            rest = [group[early:] for group in groups]
            total = sums(rest, a_at, plan, first, per, early, [total], spare)
        return total, begun

    def spread(far):
        return [one for value in far for one in halves(value[:used_rows])]

    def tied(values, *after):
        return list(lax.optimization_barrier((*values, *after)))[: len(values)]

    def partials(below, above):
        return pl.pallas_call(
            functools.partial(partial_kernel, (parts, local_rows, slots, side, meta_rows)),
            out_shape=[
                jax.ShapeDtypeStruct((lines + 10, side), jnp.float32)
            ] * parts,
            in_specs=[vectors] * 2,
            out_specs=[vectors] * parts,
            scratch_shapes=[
                pltpu.SMEM((2, meta_rows, side), jnp.float32),
                pltpu.VMEM((strip_rows, per + 1, side, side), jnp.float32),
                pltpu.SemaphoreType.DMA((2,)),
            ],
            compiler_params=pltpu.CompilerParams(vmem_limit_bytes=16 << 20),
            cost_estimate=pl.CostEstimate(flops=1, bytes_accessed=1, transcendentals=0),
            name="partials",
        )(below, above)

    own_plan = ((0, 0), (1, per), (2, 2 * per))
    below, above = shifted(upper, 1), shifted(lower, -1)
    lowers, middles, uppers = halves(lower), halves(middle), halves(upper)
    far_middle = across(middle)
    base = sums([lowers, middles, uppers], 1, own_plan, 0, slots)

    far_upper = across(upper, [base])
    far_middles = spread(far_middle)
    far_lower = across(lower, far_middles)
    all_middles = middles + far_middles
    far_uppers = spread(tied(far_upper, below, above))
    below_next, _ = strip_sums([uppers + far_uppers, all_middles], 0, ((1, per),), 0, 22)
    to_below_next = shifted_aslant(below_next, 1)

    shares = dict(enumerate(partials(*tied([below, above], below_next))))
    for bit in [1 << i for i in range(20) if (1 << i) < parts // 2]:
        shares = {
            distance: share + swapped(shares[distance ^ bit], bit)
            for distance, share in shares.items()
            if not distance & bit
        }
    far_lowers = spread(tied(far_lower, below_next)) if far_lower else []
    above_next, begun = strip_sums([lowers + far_lowers, all_middles], 0, ((1, per),), 2 * per, 9)
    far_share = across(shares[parts // 2], [begun, shares[0]]) if parts > 1 else []
    to_above_next = shifted(above_next, -1)
    if far_lowers:
        near = len(lowers)
        groups = [far_lowers, far_middles, far_uppers]
        base = sums(groups, 1, own_plan, 0, slots, near, [base])
        to_below_next = swapped(tied([to_below_next], base)[0][:lines], 1)
    middle_shares = [shares[0], *far_share]
    def finish(first, groups, result=()):
        counts = [len(group) for group in groups]
        flat = [one for group in groups for one in group]

        def kernel(base, *refs):
            ends = [sum(counts[: i + 1]) for i in range(len(counts))]
            grouped = [refs[end - count : end] for end, count in zip(ends, counts)]
            finish_kernel(first, base, *grouped, *refs[-3:])

        return pl.pallas_call(
            kernel,
            out_shape=jax.ShapeDtypeStruct(density.shape, jnp.float32),
            in_specs=[vectors] * (1 + len(flat)) + [in_hbm] * len(result),
            out_specs=in_hbm,
            scratch_shapes=[
                pltpu.VMEM((local_rows, per * len(groups), side, side), jnp.float32),
                pltpu.SemaphoreType.DMA((local_rows, per * len(groups))),
            ],
            input_output_aliases={1 + len(flat): 0} if result else {},
            compiler_params=pltpu.CompilerParams(vmem_limit_bytes=16 << 20),
            cost_estimate=pl.CostEstimate(flops=1, bytes_accessed=1, transcendentals=0),
            name="finish",
        )(base, *flat, *result)

    purified = finish(0, [[to_below_next], middle_shares])
    return finish(2 * per, [[to_above_next]], [purified])


def solution(mesh):
    return jax.shard_map(
        shards,
        mesh=mesh,
        in_specs=(
            P(("blk", "inner"), None, None, None),
            P(("blk", "inner"), None),
            P(("blk", "inner"), None, None),
        ),
        out_specs=P(("blk", "inner"), None, None, None),
        check_vma=False,
    )
```
